32 devices in a mesh: seq: 4 (over y, x), tensor: 4 (over z), fsdp: 2 (over core).
Axes of the slice: x: 2, y: 2, z: 4, core: 2. Of those that a mesh axis runs over, the one named last changes fastest.
Arguments:
- queries: bfloat16 [2, 1024, 2048], P('fsdp', 'seq', 'tensor'), may hold values from -57 to 57
- keys: bfloat16 [2, 1024, 1024], P('fsdp', 'seq', 'tensor'), may hold values from -6 to 6
- values: bfloat16 [2, 1024, 1024], P('fsdp', 'seq', 'tensor'), may hold values from -6 to 6
- cotangent: bfloat16 [2, 1024, 5376], P('fsdp', 'seq', 'tensor'), may hold values from -96 to 96
- out_weight: bfloat16 [2048, 5376], P('tensor', 'fsdp'), may hold values from -0.078125 to 0.078125
Outputs:
- query_grads: bfloat16 [2, 1024, 2048], P('fsdp', 'seq', 'tensor')
- key_grads: bfloat16 [2, 1024, 1024], P('fsdp', 'seq', 'tensor')
- value_grads: bfloat16 [2, 1024, 1024], P('fsdp', 'seq', 'tensor')
The draws below stay inside these ranges and needn't reach their ends.
All inputs are finite; a program needn't handle non-finite values.
Results may differ from the reference program's by a relative error of at most 0.015.
Values may be sent and summed in bfloat16 or wider, within the bound.
A program may use at most 64 MiB of HBM per device.

```python
import jax
import jax.numpy as jnp
from jax import lax

D = 5376
QUERY_HEADS = 16
KEY_VALUE_HEADS = 8
HEAD_SIZE = 128
WINDOW = 1024
TOK_DEV = 256
BATCH_SEQUENCES = 2
SEQUENCE_LENGTH = 1024
N_SEQ = 4


def joint_rows(key):
    query_key = jax.random.fold_in(key, 101)
    random_key_for_keys = jax.random.fold_in(key, 202)
    queries = jax.random.truncated_normal(query_key, -6.0, 6.0, (BATCH_SEQUENCES, SEQUENCE_LENGTH, QUERY_HEADS, HEAD_SIZE), jnp.float32)
    key_row_block = jax.random.truncated_normal(random_key_for_keys, -6.0, 6.0, (BATCH_SEQUENCES, SEQUENCE_LENGTH, KEY_VALUE_HEADS, HEAD_SIZE), jnp.float32)
    return (queries.reshape(BATCH_SEQUENCES, SEQUENCE_LENGTH, QUERY_HEADS * HEAD_SIZE), key_row_block.reshape(BATCH_SEQUENCES, SEQUENCE_LENGTH, KEY_VALUE_HEADS * HEAD_SIZE))


def draw_queries(key, part):
    return joint_rows(key)[0].astype(jnp.bfloat16)


def draw_keys(key, part):
    return joint_rows(key)[1].astype(jnp.bfloat16)


def steps_of(rng, shape, cuts, least, high):
    gain, own = 1.0, jax.random.fold_in(rng, 6)
    for dim, parts in cuts:
        heights = jnp.exp(jax.random.uniform(jax.random.fold_in(own, dim), (parts,), jnp.float32, least / len(cuts), high / len(cuts)))
        gain = gain * jnp.repeat(heights, shape[dim] // parts).reshape([-1 if axis == dim else 1 for axis in range(len(shape))])
    return gain


def bell_draw(rng, shape, width, bound, shards=(), kind=jnp.bfloat16):
    gain = steps_of(rng, shape, shards, -0.22, 0.18) if shards else 1.0
    entries = jax.random.normal(rng, shape, jnp.float32) * width * gain
    return jnp.minimum(jnp.maximum(entries, -bound), bound).astype(kind)


def setup_inputs(seed: int = 0) -> dict:
    seeds = jax.random.split(jax.random.key(seed), 6)
    return {
        "queries": draw_queries(jax.random.fold_in(seeds[5], 71), 0),
        "keys": draw_keys(jax.random.fold_in(seeds[5], 71), 0),
        "values": bell_draw(seeds[2], (BATCH_SEQUENCES, SEQUENCE_LENGTH, KEY_VALUE_HEADS * HEAD_SIZE), 1.0, 6.0, ((0, 2), (1, 4), (2, 4))),
        "cotangent": bell_draw(seeds[3], (BATCH_SEQUENCES, SEQUENCE_LENGTH, D), 16.0, 96.0, ((0, 2), (1, 4), (2, 4))),
        "out_weight": bell_draw(seeds[4], (QUERY_HEADS * HEAD_SIZE, D), D ** -0.5, 0.078125, ((0, 4), (1, 2))),
    }


score_scale = 168.0 ** -0.5
masked_score = -1.0e30


def window_grads(query_rows, grad_rows, key_rows, value_rows, query_places, key_places):
    rows_here = query_rows.shape[0]
    key_span = key_rows.shape[0]
    kv_heads = key_rows.shape[1] // HEAD_SIZE
    head_groups = query_rows.shape[1] // (kv_heads * HEAD_SIZE)
    q_heads = query_rows.astype(jnp.float32).reshape(rows_here, kv_heads, head_groups, HEAD_SIZE)
    g_heads = grad_rows.astype(jnp.float32).reshape(rows_here, kv_heads, head_groups, HEAD_SIZE)
    k_heads = key_rows.astype(jnp.float32).reshape(key_span, kv_heads, HEAD_SIZE)
    v_heads = value_rows.astype(jnp.float32).reshape(key_span, kv_heads, HEAD_SIZE)
    scores = jnp.einsum("tkgd,skd->kgts", q_heads, k_heads) * score_scale
    allowed = (key_places[None, :] <= query_places[:, None]) & (key_places[None, :] > query_places[:, None] - WINDOW) & (key_places[None, :] >= 0)
    scores = jnp.where(allowed, scores, masked_score)
    top_score = jnp.max(scores, axis=-1, keepdims=True)
    log_totals = top_score + jnp.log(jnp.sum(jnp.exp(scores - top_score), axis=-1, keepdims=True))
    probs = jnp.exp(scores - log_totals)
    probs_low = lax.optimization_barrier(probs.astype(jnp.bfloat16)).astype(jnp.float32)
    attended = jnp.einsum("kgts,skd->tkgd", probs_low, v_heads)
    row_terms = jnp.transpose(jnp.sum(g_heads * attended, axis=-1), (1, 2, 0))
    grad_probs = jnp.einsum("tkgd,skd->kgts", g_heads, v_heads)
    grad_scores = probs * (grad_probs - row_terms[..., None])
    grad_low = lax.optimization_barrier(grad_scores.astype(jnp.bfloat16)).astype(jnp.float32)
    part_q = jnp.einsum("kgts,skd->tkgd", grad_low, k_heads) * score_scale
    part_k = jnp.einsum("kgts,tkgd->skd", grad_low, q_heads) * score_scale
    part_v = jnp.einsum("kgts,tkgd->skd", probs_low, g_heads)
    return part_q.reshape(rows_here, -1), part_k.reshape(key_span, -1), part_v.reshape(key_span, -1)


def reference(queries, keys, values, cotangent, out_weight):
    width_q = queries.shape[2]
    width_kv = keys.shape[2]
    key_span = WINDOW + TOK_DEV
    grads_q = []
    grads_k = []
    grads_v = []
    for batch_row in range(BATCH_SEQUENCES):
        head_grads = jnp.dot(cotangent[batch_row], out_weight.T, preferred_element_type=jnp.float32).astype(jnp.bfloat16)
        key_pad = jnp.concatenate([jnp.zeros((WINDOW, width_kv), keys.dtype), keys[batch_row]], axis=0)
        value_pad = jnp.concatenate([jnp.zeros((WINDOW, width_kv), values.dtype), values[batch_row]], axis=0)
        query_all = queries[batch_row]

        def block_step(totals, block_index):
            key_acc, value_acc = totals
            first_row = (block_index * TOK_DEV).astype(jnp.int32)
            query_rows = lax.dynamic_slice_in_dim(query_all, first_row, TOK_DEV, 0)
            grad_rows = lax.dynamic_slice_in_dim(head_grads, first_row, TOK_DEV, 0)
            key_rows = lax.dynamic_slice_in_dim(key_pad, first_row, key_span, 0)
            value_rows = lax.dynamic_slice_in_dim(value_pad, first_row, key_span, 0)
            query_places = first_row + jnp.arange(TOK_DEV, dtype=jnp.int32)
            key_places = first_row - WINDOW + jnp.arange(key_span, dtype=jnp.int32)
            part_q, part_k, part_v = window_grads(query_rows, grad_rows, key_rows, value_rows, query_places, key_places)
            key_acc = lax.dynamic_update_slice_in_dim(key_acc, lax.dynamic_slice_in_dim(key_acc, first_row, key_span, 0) + part_k, first_row, 0)
            value_acc = lax.dynamic_update_slice_in_dim(value_acc, lax.dynamic_slice_in_dim(value_acc, first_row, key_span, 0) + part_v, first_row, 0)
            return (key_acc, value_acc), part_q

        zero_acc = (jnp.zeros((WINDOW + SEQUENCE_LENGTH, width_kv), jnp.float32), jnp.zeros((WINDOW + SEQUENCE_LENGTH, width_kv), jnp.float32))
        final_acc, blocks_q = lax.scan(block_step, zero_acc, jnp.arange(N_SEQ, dtype=jnp.int32))
        grads_q.append(blocks_q.reshape(SEQUENCE_LENGTH, width_q).astype(jnp.bfloat16))
        grads_k.append(final_acc[0][WINDOW:].astype(jnp.bfloat16))
        grads_v.append(final_acc[1][WINDOW:].astype(jnp.bfloat16))
    return (jnp.stack(grads_q), jnp.stack(grads_k), jnp.stack(grads_v))
```

```python
import functools

import jax
import jax.numpy as jnp
from jax import lax
from jax.experimental import pallas as pl
from jax.experimental.pallas import tpu as pltpu
from jax.sharding import PartitionSpec as P

HEAD_SIZE = 128
WINDOW = 1024
CHUNK = 128

score_scale = 168.0 ** (-0.5)
masked_score = -1e30
MESH = pl.DeviceIdType.MESH
NT = (((1,), (1,)), ((), ()))


def dot(a, b):
    return jnp.dot(a, b, preferred_element_type=jnp.float32)


def dot_nt(a, b):
    return lax.dot_general(a, b, NT, preferred_element_type=jnp.float32)


def kernel(
    n_seq, n_tensor, n_fsdp, reach,
    q_ref, k_ref, v_ref, c_ref, w_ref,
    dq_ref, dk_ref, dv_ref,
    c_all, w_all, w_cut, k_in, v_in, q_in, lse_own, lse_in, row_own, row_in, g_own, g_in,
    s_buf, p_own, p_late, att, k_turn, v_turn, top, total, turned, dq_acc, dk_acc, dv_acc,
    c_loc, w_loc, w_send, w_recv, right_send, right_recv, left_send, left_recv,
    kv_send, kv_recv, lse_send, lse_recv, g_send, g_recv,
):
    rows = q_ref.shape[0]
    kv_heads = k_ref.shape[1] // HEAD_SIZE
    groups = q_ref.shape[1] // k_ref.shape[1]
    chunks = rows // CHUNK
    features = c_ref.shape[1]
    fsdp_features = w_ref.shape[1]
    me_s, me_t, me_f = lax.axis_index("seq"), lax.axis_index("tensor"), lax.axis_index("fsdp")

    def seq_at(offset):
        return {"seq": lax.rem(me_s + offset + n_seq, n_seq)}

    def tensor_at(offset):
        return {"tensor": lax.rem(me_t + offset + n_tensor, n_tensor)}

    def fsdp_at(offset):
        return {"fsdp": lax.rem(me_f + offset + n_fsdp, n_fsdp)}

    seq_offsets = sorted({d % n_seq for r in range(1, reach + 1) for d in (r, -r)} - {0})
    tensor_offsets = sorted({1 % n_tensor, (n_tensor - 1) % n_tensor} - {0})
    peers = (
        [seq_at(d) for d in seq_offsets]
        + [tensor_at(d) for d in tensor_offsets]
        + [fsdp_at(d) for d in range(1, n_fsdp)]
    )
    barrier = pltpu.get_barrier_semaphore()
    for peer in peers:
        pl.semaphore_signal(barrier, inc=1, device_id=peer, device_id_type=MESH)
    pl.semaphore_wait(barrier, len(peers))

    def remote(src, dst, send, recv, peer):
        return pltpu.make_async_remote_copy(
            src_ref=src, dst_ref=dst, send_sem=send, recv_sem=recv,
            device_id=peer, device_id_type=MESH,
        )

    def has_earlier(d):
        return me_s >= d

    def has_later(d):
        return me_s + d < n_seq

    def right_copy(c, s):
        place = pl.ds(c * CHUNK, CHUNK)
        slot = lax.rem(me_t - s + n_tensor, n_tensor)
        src = c_ref.at[place] if s == 0 else c_all.at[slot, place]
        return remote(src, c_all.at[slot, place], right_send.at[c, s], right_recv.at[c, s], tensor_at(1))

    def left_copy(c, s):
        place = pl.ds(c * CHUNK, CHUNK)
        slot = lax.rem(me_t + s, n_tensor)
        src = c_ref.at[place] if s == 0 else c_all.at[slot, place]
        return remote(src, c_all.at[slot, place], left_send.at[c, s], left_recv.at[c, s], tensor_at(-1))

    def right_sends(s):
        return (me_t + 1 < n_tensor) & (me_t >= s)

    def left_sends(s):
        return (me_t >= 1) & (me_t + s < n_tensor)

    def w_copy(o):
        return remote(w_ref, w_all.at[me_f], w_send.at[o], w_recv.at[o], fsdp_at(o))

    def key_copies(d):
        return [
            remote(k_ref, k_in.at[d - 1], kv_send.at[0, d], kv_recv.at[0, d], seq_at(d)),
            remote(v_ref, v_in.at[d - 1], kv_send.at[1, d], kv_recv.at[1, d], seq_at(d)),
        ]

    def query_copy(d):
        return remote(q_ref, q_in.at[d - 1], kv_send.at[2, d], kv_recv.at[2, d], seq_at(-d))

    def lse_copy(d):
        return remote(lse_own, lse_in.at[d - 1], lse_send.at[d], lse_recv.at[d], seq_at(-d))

    def grad_copies(c, d):
        place = pl.ds(c * CHUNK, CHUNK)
        return [
            remote(g_own.at[place], g_in.at[d - 1, place], g_send.at[0, c, d], g_recv.at[0, c, d], seq_at(-d)),
            remote(row_own.at[c], row_in.at[c, d - 1], g_send.at[1, c, d], g_recv.at[1, c, d], seq_at(-d)),
        ]

    for c in range(chunks):
        @pl.when(right_sends(0))
        def _():
            right_copy(c, 0).start()

        @pl.when(left_sends(0))
        def _():
            left_copy(c, 0).start()
    for o in range(1, n_fsdp):
        w_copy(o).start()
    for d in range(1, reach + 1):
        @pl.when(has_later(d))
        def _():
            for copy in key_copies(d):
                copy.start()

        @pl.when(has_earlier(d))
        def _():
            query_copy(d).start()
    own_c = pltpu.make_async_copy(c_ref, c_all.at[me_t], c_loc)
    own_c.start()
    own_w = pltpu.make_async_copy(w_ref, w_all.at[me_f], w_loc)
    own_w.start()

    def lanes(h):
        return pl.ds(pl.multiple_of(h * HEAD_SIZE, HEAD_SIZE), HEAD_SIZE)

    def key_block(d):
        return k_ref if d == 0 else k_in.at[d - 1]

    def value_block(d):
        return v_ref if d == 0 else v_in.at[d - 1]

    def on_earlier(d, do):
        if d == 0:
            do()
        else:
            pl.when(has_earlier(d))(do)

    def masked(scores, d):
        shape = (rows, rows)
        if d == 0:
            j, i = lax.broadcasted_iota(jnp.int32, shape, 0), lax.broadcasted_iota(jnp.int32, shape, 1)
            return jnp.where(j <= i, scores, masked_score)
        if (d + 1) * rows - 1 >= WINDOW:
            j, i = lax.broadcasted_iota(jnp.int32, shape, 0), lax.broadcasted_iota(jnp.int32, shape, 1)
            return jnp.where(j - i > d * rows - WINDOW, scores, masked_score)
        return scores

    lse_own[...] = jnp.zeros_like(lse_own)
    row_own[...] = jnp.zeros_like(row_own)
    for d in range(1, reach + 1):
        @pl.when(has_earlier(d))
        def _():
            for copy in key_copies(d):
                copy.wait_recv()

    @pl.loop(0, kv_heads)
    def _(kv):
        for d in range(reach + 1):
            def turn():
                k_turn[kv, d] = key_block(d)[:, lanes(kv)].T
                v_turn[kv, d] = value_block(d)[:, lanes(kv)].T
            on_earlier(d, turn)
        for group in range(groups):
            h = kv * groups + group
            q = q_ref[:, lanes(h)]
            for d in range(reach + 1):
                def score():
                    scores = masked(dot_nt(key_block(d)[:, lanes(kv)], q) * score_scale, d)
                    s_buf[d] = scores
                    high = jnp.max(scores, axis=0, keepdims=True)
                    top[...] = high if d == 0 else jnp.maximum(top[...], high)
                on_earlier(d, score)
            for d in range(reach + 1):
                def add():
                    part = jnp.sum(jnp.exp(s_buf[d] - top[...]), axis=0, keepdims=True)
                    total[...] = part if d == 0 else total[...] + part
                on_earlier(d, add)
            lse = top[...] + jnp.log(total[...])
            lse_own[pl.ds(h, 1), :] = lse
            for d in range(reach + 1):
                def spread():
                    low = jnp.exp(s_buf[d] - lse_own[pl.ds(h, 1), :]).astype(jnp.bfloat16)
                    p_own[h, d] = low
                    part = dot(v_turn[kv, d], low)
                    turned[...] = part if d == 0 else turned[...] + part
                on_earlier(d, spread)
            att[h] = turned[...].T

    for d in range(1, reach + 1):
        @pl.when(has_earlier(d))
        def _():
            lse_copy(d).start()

    own_w.wait()
    for o in range(1, n_fsdp):
        w_copy(o).wait_recv()
    per_shard = fsdp_features // features
    for t in range(n_tensor):
        start = (t % per_shard) * features
        w_cut[t] = w_all[t // per_shard, :, start : start + features]

    for d in range(1, reach + 1):
        @pl.when(has_later(d))
        def _():
            query_copy(d).wait_recv()
            lse_copy(d).wait_recv()

            @pl.loop(0, kv_heads)
            def _(kv):
                for group in range(groups):
                    h = kv * groups + group
                    scores = masked(dot_nt(k_ref[:, lanes(kv)], q_in[d - 1, :, lanes(h)]) * score_scale, d)
                    p_late[h, d - 1] = jnp.exp(scores - lse_in[d - 1, pl.ds(h, 1), :]).astype(jnp.bfloat16)

    dk_acc[...] = jnp.zeros_like(dk_acc)
    dv_acc[...] = jnp.zeros_like(dv_acc)
    own_c.wait()

    def late_keys(c):
        place = pl.ds(c * CHUNK, CHUNK)
        for d in range(1, reach + 1):
            @pl.when(has_later(d))
            def _():
                for copy in grad_copies(c, d):
                    copy.wait_recv()

                @pl.loop(0, kv_heads)
                def _(kv):
                    for group in range(groups):
                        h = kv * groups + group
                        g = g_in[d - 1, place, lanes(h)]
                        probs = p_late[h, d - 1, :, place]
                        slope = dot_nt(v_ref[:, lanes(kv)], g) - row_in[c, d - 1, pl.ds(h, 1), :]
                        low = (probs.astype(jnp.float32) * slope).astype(jnp.bfloat16)
                        dk_acc[kv] += dot(low, q_in[d - 1, place, lanes(h)])
                        dv_acc[kv] += dot(probs, g)

    for c in range(chunks):
        place = pl.ds(c * CHUNK, CHUNK)
        sums = dot_nt(c_all[me_t, place], w_cut[me_t])
        for s in range(1, n_tensor):
            @pl.when(me_t >= s)
            def _():
                right_copy(c, s - 1).wait_recv()

            if s < n_tensor - 1:
                @pl.when(right_sends(s))
                def _():
                    right_copy(c, s).start()

            @pl.when(me_t + s < n_tensor)
            def _():
                left_copy(c, s - 1).wait_recv()

            if s < n_tensor - 1:
                @pl.when(left_sends(s))
                def _():
                    left_copy(c, s).start()
        for s in range(1, n_tensor):
            slot = lax.rem(me_t + s, n_tensor)
            sums += dot_nt(c_all[slot, place], w_cut[slot])
        g_own[place] = sums.astype(jnp.bfloat16)

        @pl.loop(0, kv_heads * groups)
        def _(h):
            product = g_own[place, lanes(h)].astype(jnp.float32) * att[h, place]
            row = lax.dot_general(
                jnp.ones((8, HEAD_SIZE), jnp.float32), product, NT,
                precision=lax.Precision.HIGHEST, preferred_element_type=jnp.float32,
            )
            row_own[c, pl.ds(h, 1), :] = row[0:1]

        for d in range(1, reach + 1):
            @pl.when(has_earlier(d))
            def _():
                for copy in grad_copies(c, d):
                    copy.start()

        @pl.loop(0, kv_heads)
        def _(kv):
            for group in range(groups):
                h = kv * groups + group
                g = g_own[place, lanes(h)]
                row = row_own[c, pl.ds(h, 1), :]
                for d in range(reach + 1):
                    def query_part():
                        probs = p_own[h, d, :, place]
                        slope = dot_nt(value_block(d)[:, lanes(kv)], g) - row
                        low = (probs.astype(jnp.float32) * slope).astype(jnp.bfloat16)
                        part = dot(k_turn[kv, d], low)
                        if d == 0:
                            dq_acc[...] = part
                            dk_acc[kv] += dot(low, q_ref[place, lanes(h)])
                            dv_acc[kv] += dot(probs, g)
                        else:
                            dq_acc[...] += part
                    on_earlier(d, query_part)
                dq_ref[place, lanes(h)] = (dq_acc[...] * score_scale).T.astype(jnp.bfloat16)

        if c > 0:
            late_keys(c - 1)
    late_keys(chunks - 1)
    for kv in range(kv_heads):
        lane = slice(kv * HEAD_SIZE, (kv + 1) * HEAD_SIZE)
        dk_ref[:, lane] = (dk_acc[kv] * score_scale).astype(jnp.bfloat16)
        dv_ref[:, lane] = dv_acc[kv].astype(jnp.bfloat16)

    for o in range(1, n_fsdp):
        w_copy(o).wait_send()
    for c in range(chunks):
        for s in range(n_tensor - 1):
            @pl.when(right_sends(s))
            def _():
                right_copy(c, s).wait_send()

            @pl.when(left_sends(s))
            def _():
                left_copy(c, s).wait_send()
    for d in range(1, reach + 1):
        @pl.when(has_later(d))
        def _():
            for copy in key_copies(d):
                copy.wait_send()

        @pl.when(has_earlier(d))
        def _():
            query_copy(d).wait_send()
            lse_copy(d).wait_send()
            for c in range(chunks):
                for copy in grad_copies(c, d):
                    copy.wait_send()


def per_device(mesh, queries, keys, values, cotangent, out_weight):
    n_seq, n_tensor, n_fsdp = mesh.shape["seq"], mesh.shape["tensor"], mesh.shape["fsdp"]
    q, k, v, c = queries[0], keys[0], values[0], cotangent[0]
    rows = q.shape[0]
    reach = min(WINDOW // rows, n_seq - 1)
    heads, kv_heads = q.shape[1] // HEAD_SIZE, k.shape[1] // HEAD_SIZE
    chunks = rows // CHUNK
    bf16, f32 = jnp.bfloat16, jnp.float32
    vmem = pl.BlockSpec(memory_space=pltpu.VMEM)
    hbm = pl.BlockSpec(memory_space=pl.ANY)
    dma = pltpu.SemaphoreType.DMA
    dq, dk, dv = pl.pallas_call(
        functools.partial(kernel, n_seq, n_tensor, n_fsdp, reach),
        out_shape=[jax.ShapeDtypeStruct(x.shape, bf16) for x in (q, k, v)],
        in_specs=[vmem, vmem, vmem, hbm, hbm],
        out_specs=[vmem] * 3,
        scratch_shapes=[
            pltpu.VMEM((n_tensor,) + c.shape, bf16),
            pltpu.VMEM((n_fsdp,) + out_weight.shape, bf16),
            pltpu.VMEM((n_tensor, out_weight.shape[0], c.shape[1]), bf16),
            pltpu.VMEM((reach,) + k.shape, bf16),
            pltpu.VMEM((reach,) + v.shape, bf16),
            pltpu.VMEM((reach,) + q.shape, bf16),
            pltpu.VMEM((8, rows), f32),
            pltpu.VMEM((reach, 8, rows), f32),
            pltpu.VMEM((chunks, 8, CHUNK), f32),
            pltpu.VMEM((chunks, reach, 8, CHUNK), f32),
            pltpu.VMEM(q.shape, bf16),
            pltpu.VMEM((reach,) + q.shape, bf16),
            pltpu.VMEM((reach + 1, rows, rows), f32),
            pltpu.VMEM((heads, reach + 1, rows, rows), bf16),
            pltpu.VMEM((heads, reach, rows, rows), bf16),
            pltpu.VMEM((heads, rows, HEAD_SIZE), f32),
            pltpu.VMEM((kv_heads, reach + 1, HEAD_SIZE, rows), bf16),
            pltpu.VMEM((kv_heads, reach + 1, HEAD_SIZE, rows), bf16),
            pltpu.VMEM((1, rows), f32),
            pltpu.VMEM((1, rows), f32),
            pltpu.VMEM((HEAD_SIZE, rows), f32),
            pltpu.VMEM((HEAD_SIZE, CHUNK), f32),
            pltpu.VMEM((kv_heads, rows, HEAD_SIZE), f32),
            pltpu.VMEM((kv_heads, rows, HEAD_SIZE), f32),
            dma, dma,
            dma((n_fsdp,)), dma((n_fsdp,)),
            dma((chunks, n_tensor)), dma((chunks, n_tensor)),
            dma((chunks, n_tensor)), dma((chunks, n_tensor)),
            dma((3, reach + 1)), dma((3, reach + 1)),
            dma((reach + 1,)), dma((reach + 1,)),
            dma((2, chunks, reach + 1)), dma((2, chunks, reach + 1)),
        ],
        compiler_params=pltpu.CompilerParams(
            collective_id=0, has_side_effects=True, vmem_limit_bytes=56 * 2**20
        ),
        cost_estimate=pl.CostEstimate(flops=4 * 10**9, bytes_accessed=8 * 10**6, transcendentals=4 * 10**6),
    )(q, k, v, c, out_weight)
    return dq[None], dk[None], dv[None]


def solution(mesh):
    parts = P("fsdp", "seq", "tensor")
    return jax.shard_map(
        functools.partial(per_device, mesh),
        mesh=mesh,
        in_specs=(parts, parts, parts, parts, P("tensor", "fsdp")),
        out_specs=(parts, parts, parts),
        check_vma=False,
    )
```

```python
import functools

import jax
import jax.numpy as jnp
from jax import lax
from jax.experimental import pallas as pl
from jax.experimental.pallas import tpu as pltpu
from jax.sharding import PartitionSpec as P

HEAD_SIZE = 128
WINDOW = 1024
CHUNK = 128

score_scale = 168.0 ** (-0.5)
masked_score = -1e30
MESH = pl.DeviceIdType.MESH
NT = (((1,), (1,)), ((), ()))


def dot(a, b):
    return jnp.dot(a, b, preferred_element_type=jnp.float32)


def dot_nt(a, b):
    return lax.dot_general(a, b, NT, preferred_element_type=jnp.float32)


def kernel(
    n_seq, n_tensor, n_fsdp, reach,
    q_ref, k_ref, v_ref, c_ref, w_ref,
    dq_ref, dk_ref, dv_ref,
    c_all, w_all, k_in, v_in, q_in, lse_own, lse_in, row_own, row_in, g_own, g_in,
    s_buf, p_own, p_late, att, k_turn, v_turn, top, total, turned, dq_acc, dk_acc, dv_acc,
    c_loc, w_loc, w_send, w_recv, right_send, right_recv, left_send, left_recv,
    kv_send, kv_recv, lse_send, lse_recv, g_send, g_recv,
):
    rows = q_ref.shape[0]
    kv_heads = k_ref.shape[1] // HEAD_SIZE
    groups = q_ref.shape[1] // k_ref.shape[1]
    chunks = rows // CHUNK
    features = c_ref.shape[0]
    fsdp_features = w_ref.shape[1]
    me_s, me_t, me_f = lax.axis_index("seq"), lax.axis_index("tensor"), lax.axis_index("fsdp")

    def seq_at(offset):
        return {"seq": lax.rem(me_s + offset + n_seq, n_seq)}

    def tensor_at(offset):
        return {"tensor": lax.rem(me_t + offset + n_tensor, n_tensor)}

    def fsdp_at(offset):
        return {"fsdp": lax.rem(me_f + offset + n_fsdp, n_fsdp)}

    seq_offsets = sorted({d % n_seq for r in range(1, reach + 1) for d in (r, -r)} - {0})
    tensor_offsets = sorted({1 % n_tensor, (n_tensor - 1) % n_tensor} - {0})
    peers = (
        [seq_at(d) for d in seq_offsets]
        + [tensor_at(d) for d in tensor_offsets]
        + [fsdp_at(d) for d in range(1, n_fsdp)]
    )
    barrier = pltpu.get_barrier_semaphore()
    for peer in peers:
        pl.semaphore_signal(barrier, inc=1, device_id=peer, device_id_type=MESH)
    pl.semaphore_wait(barrier, len(peers))

    def remote(src, dst, send, recv, peer):
        return pltpu.make_async_remote_copy(
            src_ref=src, dst_ref=dst, send_sem=send, recv_sem=recv,
            device_id=peer, device_id_type=MESH,
        )

    def has_earlier(d):
        return me_s >= d

    def has_later(d):
        return me_s + d < n_seq

    def block(slot):
        return pl.ds(pl.multiple_of(slot * features, 16), features)

    def right_copy(c, s):
        place = pl.ds(c * CHUNK, CHUNK)
        slot = lax.rem(me_t - s + n_tensor, n_tensor)
        there = c_all.at[block(slot), place]
        src = c_ref.at[:, place] if s == 0 else there
        return remote(src, there, right_send.at[c, s], right_recv.at[c, s], tensor_at(1))

    def left_copy(c, s):
        place = pl.ds(c * CHUNK, CHUNK)
        slot = lax.rem(me_t + s, n_tensor)
        there = c_all.at[block(slot), place]
        src = c_ref.at[:, place] if s == 0 else there
        return remote(src, there, left_send.at[c, s], left_recv.at[c, s], tensor_at(-1))

    def right_sends(s):
        return (me_t + 1 < n_tensor) & (me_t >= s)

    def left_sends(s):
        return (me_t >= 1) & (me_t + s < n_tensor)

    def w_copy(o):
        return remote(w_ref, w_all.at[me_f], w_send.at[o], w_recv.at[o], fsdp_at(o))

    def key_copies(d):
        return [
            remote(k_ref, k_in.at[d - 1], kv_send.at[0, d], kv_recv.at[0, d], seq_at(d)),
            remote(v_ref, v_in.at[d - 1], kv_send.at[1, d], kv_recv.at[1, d], seq_at(d)),
        ]

    def query_copy(d):
        return remote(q_ref, q_in.at[d - 1], kv_send.at[2, d], kv_recv.at[2, d], seq_at(-d))

    def lse_copy(d):
        return remote(lse_own, lse_in.at[d - 1], lse_send.at[d], lse_recv.at[d], seq_at(-d))

    def grad_copies(c, d):
        place = pl.ds(c * CHUNK, CHUNK)
        return [
            remote(g_own.at[:, place], g_in.at[d - 1, :, place], g_send.at[0, c, d], g_recv.at[0, c, d], seq_at(-d)),
            remote(row_own.at[c], row_in.at[c, d - 1], g_send.at[1, c, d], g_recv.at[1, c, d], seq_at(-d)),
        ]

    for c in range(chunks):
        @pl.when(right_sends(0))
        def _():
            right_copy(c, 0).start()

        @pl.when(left_sends(0))
        def _():
            left_copy(c, 0).start()
    for o in range(1, n_fsdp):
        w_copy(o).start()
    for d in range(1, reach + 1):
        @pl.when(has_later(d))
        def _():
            for copy in key_copies(d):
                copy.start()

        @pl.when(has_earlier(d))
        def _():
            query_copy(d).start()

    def pump(c, s):
        @pl.when(me_t >= s)
        def _():
            right_copy(c, s - 1).wait_recv()

        if s < n_tensor - 1:
            @pl.when(right_sends(s))
            def _():
                right_copy(c, s).start()

        @pl.when(me_t + s < n_tensor)
        def _():
            left_copy(c, s - 1).wait_recv()

        if s < n_tensor - 1:
            @pl.when(left_sends(s))
            def _():
                left_copy(c, s).start()

    pumped = []

    def pump_next(count):
        order = [(c, s) for s in range(1, min(3, n_tensor)) for c in range(chunks)]
        order += [(c, s) for c in range(chunks) for s in range(3, n_tensor)]
        for c, s in order[len(pumped) : len(pumped) + count]:
            pump(c, s)
            pumped.append((c, s))

    own_c = pltpu.make_async_copy(c_ref, c_all.at[block(me_t)], c_loc)
    own_c.start()
    own_w = pltpu.make_async_copy(w_ref, w_all.at[me_f], w_loc)
    own_w.start()

    def lanes(h):
        return pl.ds(pl.multiple_of(h * HEAD_SIZE, HEAD_SIZE), HEAD_SIZE)

    def key_block(d):
        return k_ref if d == 0 else k_in.at[d - 1]

    def value_block(d):
        return v_ref if d == 0 else v_in.at[d - 1]

    def on_earlier(d, do):
        if d == 0:
            do()
        else:
            pl.when(has_earlier(d))(do)

    def masked(scores, d):
        shape = (rows, rows)
        if d == 0:
            j, i = lax.broadcasted_iota(jnp.int32, shape, 0), lax.broadcasted_iota(jnp.int32, shape, 1)
            return jnp.where(j <= i, scores, masked_score)
        if (d + 1) * rows - 1 >= WINDOW:
            j, i = lax.broadcasted_iota(jnp.int32, shape, 0), lax.broadcasted_iota(jnp.int32, shape, 1)
            return jnp.where(j - i > d * rows - WINDOW, scores, masked_score)
        return scores

    pump_next(1)
    lse_own[...] = jnp.zeros_like(lse_own)
    row_own[...] = jnp.zeros_like(row_own)
    for d in range(1, reach + 1):
        @pl.when(has_earlier(d))
        def _():
            for copy in key_copies(d):
                copy.wait_recv()

    @pl.loop(0, kv_heads)
    def _(kv):
        for d in range(reach + 1):
            def turn():
                k_turn[kv, d] = key_block(d)[:, lanes(kv)].T
                v_turn[kv, d] = value_block(d)[:, lanes(kv)].T
            on_earlier(d, turn)
        for group in range(groups):
            h = kv * groups + group
            q = q_ref[:, lanes(h)]
            for d in range(reach + 1):
                def score():
                    scores = masked(dot_nt(key_block(d)[:, lanes(kv)], q) * score_scale, d)
                    s_buf[d] = scores
                    high = jnp.max(scores, axis=0, keepdims=True)
                    top[...] = high if d == 0 else jnp.maximum(top[...], high)
                on_earlier(d, score)
            for d in range(reach + 1):
                def add():
                    part = jnp.sum(jnp.exp(s_buf[d] - top[...]), axis=0, keepdims=True)
                    total[...] = part if d == 0 else total[...] + part
                on_earlier(d, add)
            lse = top[...] + jnp.log(total[...])
            lse_own[pl.ds(h, 1), :] = lse
            for d in range(reach + 1):
                def spread():
                    low = jnp.exp(s_buf[d] - lse_own[pl.ds(h, 1), :]).astype(jnp.bfloat16)
                    p_own[h, d] = low
                    part = dot(v_turn[kv, d], low)
                    turned[...] = part if d == 0 else turned[...] + part
                on_earlier(d, spread)
            att[h] = turned[...]

    for d in range(1, reach + 1):
        @pl.when(has_earlier(d))
        def _():
            lse_copy(d).start()

    pump_next(1)

    own_w.wait()
    for o in range(1, n_fsdp):
        w_copy(o).wait_recv()
    pump_next(1)

    for d in range(1, reach + 1):
        @pl.when(has_later(d))
        def _():
            query_copy(d).wait_recv()
            lse_copy(d).wait_recv()

            @pl.loop(0, kv_heads)
            def _(kv):
                for group in range(groups):
                    h = kv * groups + group
                    scores = masked(dot_nt(k_ref[:, lanes(kv)], q_in[d - 1, :, lanes(h)]) * score_scale, d)
                    p_late[h, d - 1] = jnp.exp(scores - lse_in[d - 1, pl.ds(h, 1), :]).astype(jnp.bfloat16)

    dk_acc[...] = jnp.zeros_like(dk_acc)
    dv_acc[...] = jnp.zeros_like(dv_acc)
    own_c.wait()

    def late_keys(c):
        place = pl.ds(c * CHUNK, CHUNK)
        for d in range(1, reach + 1):
            @pl.when(has_later(d))
            def _():
                for copy in grad_copies(c, d):
                    copy.wait_recv()

                @pl.loop(0, kv_heads)
                def _(kv):
                    for group in range(groups):
                        h = kv * groups + group
                        g = g_in[d - 1, lanes(h), place]
                        probs = p_late[h, d - 1, :, place]
                        slope = dot(v_ref[:, lanes(kv)], g) - row_in[c, d - 1, pl.ds(h, 1), :]
                        low = (probs.astype(jnp.float32) * slope).astype(jnp.bfloat16)
                        dk_acc[kv] += dot(low, q_in[d - 1, place, lanes(h)])
                        dv_acc[kv] += dot_nt(probs, g)

    for c in range(chunks):
        place = pl.ds(c * CHUNK, CHUNK)
        while not all((c, s) in pumped for s in range(1, n_tensor)):
            pump_next(1)
        sums = dot(w_all[0], c_all[:fsdp_features, place])
        for f in range(1, n_fsdp):
            sums += dot(w_all[f], c_all[f * fsdp_features : (f + 1) * fsdp_features, place])
        g_own[:, place] = sums.astype(jnp.bfloat16)

        @pl.loop(0, kv_heads * groups)
        def _(h):
            product = g_own[lanes(h), place].astype(jnp.float32) * att[h, :, place]
            row_own[c, pl.ds(h, 1), :] = jnp.sum(product, axis=0, keepdims=True)

        for d in range(1, reach + 1):
            @pl.when(has_earlier(d))
            def _():
                for copy in grad_copies(c, d):
                    copy.start()

        @pl.loop(0, kv_heads)
        def _(kv):
            for group in range(groups):
                h = kv * groups + group
                g = g_own[lanes(h), place]
                row = row_own[c, pl.ds(h, 1), :]
                for d in range(reach + 1):
                    def query_part():
                        probs = p_own[h, d, :, place]
                        slope = dot(value_block(d)[:, lanes(kv)], g) - row
                        low = (probs.astype(jnp.float32) * slope).astype(jnp.bfloat16)
                        part = dot(k_turn[kv, d], low)
                        if d == 0:
                            dq_acc[...] = part
                            dk_acc[kv] += dot(low, q_ref[place, lanes(h)])
                            dv_acc[kv] += dot_nt(probs, g)
                        else:
                            dq_acc[...] += part
                    on_earlier(d, query_part)
                dq_ref[place, lanes(h)] = (dq_acc[...] * score_scale).T.astype(jnp.bfloat16)

        if c > 0:
            late_keys(c - 1)
    late_keys(chunks - 1)
    for kv in range(kv_heads):
        lane = slice(kv * HEAD_SIZE, (kv + 1) * HEAD_SIZE)
        dk_ref[:, lane] = (dk_acc[kv] * score_scale).astype(jnp.bfloat16)
        dv_ref[:, lane] = dv_acc[kv].astype(jnp.bfloat16)

    for o in range(1, n_fsdp):
        w_copy(o).wait_send()
    for c in range(chunks):
        for s in range(n_tensor - 1):
            @pl.when(right_sends(s))
            def _():
                right_copy(c, s).wait_send()

            @pl.when(left_sends(s))
            def _():
                left_copy(c, s).wait_send()
    for d in range(1, reach + 1):
        @pl.when(has_later(d))
        def _():
            for copy in key_copies(d):
                copy.wait_send()

        @pl.when(has_earlier(d))
        def _():
            query_copy(d).wait_send()
            lse_copy(d).wait_send()
            for c in range(chunks):
                for copy in grad_copies(c, d):
                    copy.wait_send()


def place_kernel(a_in, b_in, c_in, a_out, b_out, c_out, sems):
    copies = [
        pltpu.make_async_copy(src, dst, sems.at[i])
        for i, (src, dst) in enumerate(((a_in, a_out), (b_in, b_out), (c_in, c_out)))
    ]
    for copy in copies:
        copy.start()
    for copy in copies:
        copy.wait()


def per_device(mesh, queries, keys, values, cotangent, out_weight):
    n_seq, n_tensor, n_fsdp = mesh.shape["seq"], mesh.shape["tensor"], mesh.shape["fsdp"]
    q, k, v, c = queries[0], keys[0], values[0], cotangent[0].T
    rows = q.shape[0]
    reach = min(WINDOW // rows, n_seq - 1)
    heads, kv_heads = q.shape[1] // HEAD_SIZE, k.shape[1] // HEAD_SIZE
    chunks = rows // CHUNK
    bf16, f32 = jnp.bfloat16, jnp.float32
    vmem = pl.BlockSpec(memory_space=pltpu.VMEM)
    hbm = pl.BlockSpec(memory_space=pl.ANY)
    dma = pltpu.SemaphoreType.DMA
    dq, dk, dv = pl.pallas_call(
        functools.partial(kernel, n_seq, n_tensor, n_fsdp, reach),
        out_shape=[jax.ShapeDtypeStruct(x.shape, bf16) for x in (q, k, v)],
        in_specs=[vmem, vmem, vmem, hbm, hbm],
        out_specs=[vmem] * 3,
        scratch_shapes=[
            pltpu.VMEM((n_tensor * c.shape[0], rows), bf16),
            pltpu.VMEM((n_fsdp,) + out_weight.shape, bf16),
            pltpu.VMEM((reach,) + k.shape, bf16),
            pltpu.VMEM((reach,) + v.shape, bf16),
            pltpu.VMEM((reach,) + q.shape, bf16),
            pltpu.VMEM((8, rows), f32),
            pltpu.VMEM((reach, 8, rows), f32),
            pltpu.VMEM((chunks, 8, CHUNK), f32),
            pltpu.VMEM((chunks, reach, 8, CHUNK), f32),
            pltpu.VMEM(q.shape[::-1], bf16),
            pltpu.VMEM((reach,) + q.shape[::-1], bf16),
            pltpu.VMEM((reach + 1, rows, rows), f32),
            pltpu.VMEM((heads, reach + 1, rows, rows), bf16),
            pltpu.VMEM((heads, reach, rows, rows), bf16),
            pltpu.VMEM((heads, HEAD_SIZE, rows), f32),
            pltpu.VMEM((kv_heads, reach + 1, HEAD_SIZE, rows), bf16),
            pltpu.VMEM((kv_heads, reach + 1, HEAD_SIZE, rows), bf16),
            pltpu.VMEM((1, rows), f32),
            pltpu.VMEM((1, rows), f32),
            pltpu.VMEM((HEAD_SIZE, rows), f32),
            pltpu.VMEM((HEAD_SIZE, CHUNK), f32),
            pltpu.VMEM((kv_heads, rows, HEAD_SIZE), f32),
            pltpu.VMEM((kv_heads, rows, HEAD_SIZE), f32),
            dma, dma,
            dma((n_fsdp,)), dma((n_fsdp,)),
            dma((chunks, n_tensor)), dma((chunks, n_tensor)),
            dma((chunks, n_tensor)), dma((chunks, n_tensor)),
            dma((3, reach + 1)), dma((3, reach + 1)),
            dma((reach + 1,)), dma((reach + 1,)),
            dma((2, chunks, reach + 1)), dma((2, chunks, reach + 1)),
        ],
        compiler_params=pltpu.CompilerParams(
            collective_id=0, has_side_effects=True, vmem_limit_bytes=56 * 2**20
        ),
        cost_estimate=pl.CostEstimate(flops=4 * 10**9, bytes_accessed=8 * 10**6, transcendentals=4 * 10**6),
    )(q, k, v, c, out_weight)
    dq, dk, dv = pl.pallas_call(
        place_kernel,
        out_shape=[jax.ShapeDtypeStruct(x.shape, bf16) for x in (q, k, v)],
        in_specs=[hbm] * 3,
        out_specs=[hbm] * 3,
        scratch_shapes=[dma((3,))],
    )(dq, dk, dv)
    return dq[None], dk[None], dv[None]


def solution(mesh):
    parts = P("fsdp", "seq", "tensor")
    return jax.shard_map(
        functools.partial(per_device, mesh),
        mesh=mesh,
        in_specs=(parts, parts, parts, parts, P("tensor", "fsdp")),
        out_specs=(parts, parts, parts),
        check_vma=False,
    )
```

```python
import functools

import jax
import jax.numpy as jnp
from jax import lax
from jax.experimental import pallas as pl
from jax.experimental.pallas import tpu as pltpu
from jax.sharding import PartitionSpec as P

HEAD_SIZE = 128
WINDOW = 1024
CHUNK = 128

score_scale = 168.0 ** (-0.5)
masked_score = -1e30
MESH = pl.DeviceIdType.MESH
NT = (((1,), (1,)), ((), ()))


def dot(a, b):
    return jnp.dot(a, b, preferred_element_type=jnp.float32)


def dot_nt(a, b):
    return lax.dot_general(a, b, NT, preferred_element_type=jnp.float32)


def is_lean(n_seq, n_tensor, n_fsdp, reach):
    return n_tensor == 4 and n_fsdp == 2 and n_seq > 1 and reach == n_seq - 1


def kernel(
    n_seq, n_tensor, n_fsdp, reach,
    q_ref, k_ref, v_ref, c_ref, w_ref,
    dq_ref, dk_ref, dv_ref,
    c_all, w_all, k_in, v_in, q_in, lse_own, lse_in, row_own, row_in, g_own, g_in,
    s_buf, p_own, p_late, att, k_turn, v_turn, top, total, turned, dq_acc, dk_acc, dv_acc,
    w_far, part_out, part_in,
    c_loc, w_loc, w_send, w_recv, right_send, right_recv, left_send, left_recv,
    kv_send, kv_recv, lse_send, lse_recv, g_send, g_recv,
    far_send, far_recv, pass_send, pass_recv, part_send, part_recv,
):
    rows = q_ref.shape[0]
    kv_heads = k_ref.shape[1] // HEAD_SIZE
    groups = q_ref.shape[1] // k_ref.shape[1]
    chunks = rows // CHUNK
    features = c_ref.shape[0]
    fsdp_features = w_ref.shape[1]
    me_s, me_t, me_f = lax.axis_index("seq"), lax.axis_index("tensor"), lax.axis_index("fsdp")

    def seq_at(offset):
        return {"seq": lax.rem(me_s + offset + n_seq, n_seq)}

    def tensor_at(offset):
        return {"tensor": lax.rem(me_t + offset + n_tensor, n_tensor)}

    def fsdp_at(offset):
        return {"fsdp": lax.rem(me_f + offset + n_fsdp, n_fsdp)}

    seq_offsets = sorted({d % n_seq for r in range(1, reach + 1) for d in (r, -r)} - {0})
    tensor_offsets = sorted({1 % n_tensor, (n_tensor - 1) % n_tensor} - {0})
    peers = (
        [seq_at(d) for d in seq_offsets]
        + [tensor_at(d) for d in tensor_offsets]
        + [fsdp_at(d) for d in range(1, n_fsdp)]
    )
    barrier = pltpu.get_barrier_semaphore()
    for peer in peers:
        pl.semaphore_signal(barrier, inc=1, device_id=peer, device_id_type=MESH)
    pl.semaphore_wait(barrier, len(peers))

    def remote(src, dst, send, recv, peer):
        return pltpu.make_async_remote_copy(
            src_ref=src, dst_ref=dst, send_sem=send, recv_sem=recv,
            device_id=peer, device_id_type=MESH,
        )

    def has_earlier(d):
        return me_s >= d

    def has_later(d):
        return me_s + d < n_seq

    def block(slot):
        return pl.ds(pl.multiple_of(slot * features, 16), features)

    def right_copy(c, s):
        place = pl.ds(c * CHUNK, CHUNK)
        slot = lax.rem(me_t - s + n_tensor, n_tensor)
        there = c_all.at[block(slot), place]
        src = c_ref.at[:, place] if s == 0 else there
        return remote(src, there, right_send.at[c, s], right_recv.at[c, s], tensor_at(1))

    def left_copy(c, s):
        place = pl.ds(c * CHUNK, CHUNK)
        slot = lax.rem(me_t + s, n_tensor)
        there = c_all.at[block(slot), place]
        src = c_ref.at[:, place] if s == 0 else there
        return remote(src, there, left_send.at[c, s], left_recv.at[c, s], tensor_at(-1))

    lean = is_lean(n_seq, n_tensor, n_fsdp, reach)
    is_end = (me_t == 0) | (me_t == 3)
    is_helper = (me_t == 1) | (me_t == 2)
    far_shard = 1 - lax.div(me_t, 2)
    gives_far = is_end & (me_f == far_shard)
    holds_far = is_helper & (me_f == far_shard)
    takes_far = is_helper & (me_f != far_shard)

    def far_rows(offset):
        quarter = w_ref.shape[0] // n_seq
        piece = lax.rem(me_s - offset + n_seq, n_seq)
        return pl.ds(pl.multiple_of(piece * quarter, 16), quarter)

    def far_first():
        place = far_rows(0)
        return remote(w_ref.at[place], w_far.at[place], far_send.at[0], far_recv.at[0],
                      {"tensor": 1 + lax.div(me_t, 3)})

    def far_share(d):
        place = far_rows(0)
        return remote(w_far.at[place], w_far.at[place], far_send.at[d], far_recv.at[d], seq_at(d))

    def far_pass(d):
        place = far_rows(d)
        return remote(w_far.at[place], w_far.at[place], pass_send.at[d], pass_recv.at[d], fsdp_at(1))

    def part_copy(c):
        place = pl.ds(c * CHUNK, CHUNK)
        return remote(part_out.at[:, place], part_in.at[:, place], part_send.at[c], part_recv.at[c],
                      {"tensor": 3 * lax.div(me_t, 2)})

    def right_sends(s):
        if lean and s > 0:
            return me_t == 1
        return (me_t + 1 < n_tensor) & (me_t >= s)

    def left_sends(s):
        if lean and s > 0:
            return me_t == 2
        return (me_t >= 1) & (me_t + s < n_tensor)

    def right_lands(s):
        return me_t == 2 if lean and s > 1 else me_t >= s

    def left_lands(s):
        return me_t == 1 if lean and s > 1 else me_t + s < n_tensor

    hops = 3 if lean else n_tensor

    def w_copy(o):
        return remote(w_ref, w_all.at[me_f], w_send.at[o], w_recv.at[o], fsdp_at(o))

    def key_copies(d):
        return [
            remote(k_ref, k_in.at[d - 1], kv_send.at[0, d], kv_recv.at[0, d], seq_at(d)),
            remote(v_ref, v_in.at[d - 1], kv_send.at[1, d], kv_recv.at[1, d], seq_at(d)),
        ]

    def query_copy(d):
        return remote(q_ref, q_in.at[d - 1], kv_send.at[2, d], kv_recv.at[2, d], seq_at(-d))

    def lse_copy(d):
        return remote(lse_own, lse_in.at[d - 1], lse_send.at[d], lse_recv.at[d], seq_at(-d))

    def grad_copies(c, d):
        place = pl.ds(c * CHUNK, CHUNK)
        return [
            remote(g_own.at[:, place], g_in.at[d - 1, :, place], g_send.at[0, c, d], g_recv.at[0, c, d], seq_at(-d)),
            remote(row_own.at[c], row_in.at[c, d - 1], g_send.at[1, c, d], g_recv.at[1, c, d], seq_at(-d)),
        ]

    for c in range(chunks):
        @pl.when(right_sends(0))
        def _():
            right_copy(c, 0).start()

        @pl.when(left_sends(0))
        def _():
            left_copy(c, 0).start()

        if lean and c == 0:
            @pl.when(gives_far)
            def _():
                far_first().start()
    for o in range(1, n_fsdp):
        w_copy(o).start()
    for d in range(1, reach + 1):
        @pl.when(has_later(d))
        def _():
            for copy in key_copies(d):
                copy.start()

        @pl.when(has_earlier(d))
        def _():
            query_copy(d).start()

    def pump(c, s):
        @pl.when(right_lands(s))
        def _():
            right_copy(c, s - 1).wait_recv()

        if s < hops - 1:
            @pl.when(right_sends(s))
            def _():
                right_copy(c, s).start()

        @pl.when(left_lands(s))
        def _():
            left_copy(c, s - 1).wait_recv()

        if s < hops - 1:
            @pl.when(left_sends(s))
            def _():
                left_copy(c, s).start()

    pumped = []

    def pump_next(count):
        order = [(c, s) for s in range(1, min(3, hops)) for c in range(chunks)]
        order += [(c, s) for c in range(chunks) for s in range(3, hops)]
        for c, s in order[len(pumped) : len(pumped) + count]:
            pump(c, s)
            pumped.append((c, s))

    own_c = pltpu.make_async_copy(c_ref, c_all.at[block(me_t)], c_loc)
    own_c.start()
    own_w = pltpu.make_async_copy(w_ref, w_all.at[me_f], w_loc)
    own_w.start()

    def lanes(h):
        return pl.ds(pl.multiple_of(h * HEAD_SIZE, HEAD_SIZE), HEAD_SIZE)

    def key_block(d):
        return k_ref if d == 0 else k_in.at[d - 1]

    def value_block(d):
        return v_ref if d == 0 else v_in.at[d - 1]

    def on_earlier(d, do):
        if d == 0:
            do()
        else:
            pl.when(has_earlier(d))(do)

    def masked(scores, d):
        shape = (rows, rows)
        if d == 0:
            j, i = lax.broadcasted_iota(jnp.int32, shape, 0), lax.broadcasted_iota(jnp.int32, shape, 1)
            return jnp.where(j <= i, scores, masked_score)
        if (d + 1) * rows - 1 >= WINDOW:
            j, i = lax.broadcasted_iota(jnp.int32, shape, 0), lax.broadcasted_iota(jnp.int32, shape, 1)
            return jnp.where(j - i > d * rows - WINDOW, scores, masked_score)
        return scores

    pump_next(1)
    lse_own[...] = jnp.zeros_like(lse_own)
    row_own[...] = jnp.zeros_like(row_own)
    for d in range(1, reach + 1):
        @pl.when(has_earlier(d))
        def _():
            for copy in key_copies(d):
                copy.wait_recv()

    @pl.loop(0, kv_heads)
    def _(kv):
        for d in range(reach + 1):
            def turn():
                k_turn[kv, d] = key_block(d)[:, lanes(kv)].T
                v_turn[kv, d] = value_block(d)[:, lanes(kv)].T
            on_earlier(d, turn)
        for group in range(groups):
            h = kv * groups + group
            q = q_ref[:, lanes(h)]
            for d in range(reach + 1):
                def score():
                    scores = masked(dot_nt(key_block(d)[:, lanes(kv)], q) * score_scale, d)
                    s_buf[d] = scores
                    high = jnp.max(scores, axis=0, keepdims=True)
                    top[...] = high if d == 0 else jnp.maximum(top[...], high)
                on_earlier(d, score)
            for d in range(reach + 1):
                def add():
                    part = jnp.sum(jnp.exp(s_buf[d] - top[...]), axis=0, keepdims=True)
                    total[...] = part if d == 0 else total[...] + part
                on_earlier(d, add)
            lse = top[...] + jnp.log(total[...])
            lse_own[pl.ds(h, 1), :] = lse
            for d in range(reach + 1):
                def spread():
                    low = jnp.exp(s_buf[d] - lse_own[pl.ds(h, 1), :]).astype(jnp.bfloat16)
                    p_own[h, d] = low
                    part = dot(v_turn[kv, d], low)
                    turned[...] = part if d == 0 else turned[...] + part
                on_earlier(d, spread)
            att[h] = turned[...]

    for d in range(1, reach + 1):
        @pl.when(has_earlier(d))
        def _():
            lse_copy(d).start()

    pump_next(1)

    if lean:
        @pl.when(holds_far)
        def _():
            far_first().wait_recv()
            for d in range(1, n_seq):
                far_share(d).start()
            far_pass(0).start()

    own_w.wait()
    for o in range(1, n_fsdp):
        w_copy(o).wait_recv()
    pump_next(1)

    for d in range(1, reach + 1):
        @pl.when(has_later(d))
        def _():
            query_copy(d).wait_recv()
            lse_copy(d).wait_recv()

            @pl.loop(0, kv_heads)
            def _(kv):
                for group in range(groups):
                    h = kv * groups + group
                    scores = masked(dot_nt(k_ref[:, lanes(kv)], q_in[d - 1, :, lanes(h)]) * score_scale, d)
                    p_late[h, d - 1] = jnp.exp(scores - lse_in[d - 1, pl.ds(h, 1), :]).astype(jnp.bfloat16)

    if lean:
        @pl.when(holds_far)
        def _():
            for d in range(1, n_seq):
                far_share(d).wait_recv()
                far_pass(d).start()

        @pl.when(takes_far)
        def _():
            for d in range(n_seq):
                far_pass(d).wait_recv()

    dk_acc[...] = jnp.zeros_like(dk_acc)
    dv_acc[...] = jnp.zeros_like(dv_acc)
    own_c.wait()

    def late_keys(c):
        place = pl.ds(c * CHUNK, CHUNK)
        for d in range(1, reach + 1):
            @pl.when(has_later(d))
            def _():
                for copy in grad_copies(c, d):
                    copy.wait_recv()

                @pl.loop(0, kv_heads)
                def _(kv):
                    for group in range(groups):
                        h = kv * groups + group
                        g = g_in[d - 1, lanes(h), place]
                        probs = p_late[h, d - 1, :, place]
                        slope = dot(v_ref[:, lanes(kv)], g) - row_in[c, d - 1, pl.ds(h, 1), :]
                        low = (probs.astype(jnp.float32) * slope).astype(jnp.bfloat16)
                        dk_acc[kv] += dot(low, q_in[d - 1, place, lanes(h)])
                        dv_acc[kv] += dot_nt(probs, g)

    for c in range(chunks):
        place = pl.ds(c * CHUNK, CHUNK)
        while not all((c, s) in pumped for s in range(1, hops)):
            pump_next(1)
        def full_sums():
            sums = dot(w_all[0], c_all[:fsdp_features, place])
            for f in range(1, n_fsdp):
                sums += dot(w_all[f], c_all[f * fsdp_features : (f + 1) * fsdp_features, place])
            g_own[:, place] = sums.astype(jnp.bfloat16)

        def shard_features(f):
            return pl.ds(pl.multiple_of(f * fsdp_features, 16), fsdp_features)

        if lean:
            @pl.when(is_helper)
            def _():
                part = dot(w_far[...], c_all[shard_features(far_shard), place])
                part_out[:, place] = part.astype(jnp.bfloat16)
                part_copy(c).start()
                full_sums()

            @pl.when(is_end)
            def _():
                near = 1 - far_shard
                sums = dot(w_all[near], c_all[shard_features(near), place])
                part_copy(c).wait_recv()
                g_own[:, place] = (sums + part_in[:, place].astype(jnp.float32)).astype(jnp.bfloat16)
        else:
            full_sums()

        @pl.loop(0, kv_heads * groups)
        def _(h):
            product = g_own[lanes(h), place].astype(jnp.float32) * att[h, :, place]
            row_own[c, pl.ds(h, 1), :] = jnp.sum(product, axis=0, keepdims=True)

        for d in range(1, reach + 1):
            @pl.when(has_earlier(d))
            def _():
                for copy in grad_copies(c, d):
                    copy.start()

        @pl.loop(0, kv_heads)
        def _(kv):
            for group in range(groups):
                h = kv * groups + group
                g = g_own[lanes(h), place]
                row = row_own[c, pl.ds(h, 1), :]
                for d in range(reach + 1):
                    def query_part():
                        probs = p_own[h, d, :, place]
                        slope = dot(value_block(d)[:, lanes(kv)], g) - row
                        low = (probs.astype(jnp.float32) * slope).astype(jnp.bfloat16)
                        part = dot(k_turn[kv, d], low)
                        if d == 0:
                            dq_acc[...] = part
                            dk_acc[kv] += dot(low, q_ref[place, lanes(h)])
                            dv_acc[kv] += dot_nt(probs, g)
                        else:
                            dq_acc[...] += part
                    on_earlier(d, query_part)
                dq_ref[place, lanes(h)] = (dq_acc[...] * score_scale).T.astype(jnp.bfloat16)

        if c > 0:
            late_keys(c - 1)
    late_keys(chunks - 1)
    for kv in range(kv_heads):
        lane = slice(kv * HEAD_SIZE, (kv + 1) * HEAD_SIZE)
        dk_ref[:, lane] = (dk_acc[kv] * score_scale).astype(jnp.bfloat16)
        dv_ref[:, lane] = dv_acc[kv].astype(jnp.bfloat16)

    for o in range(1, n_fsdp):
        w_copy(o).wait_send()
    if lean:
        @pl.when(gives_far)
        def _():
            far_first().wait_send()

        @pl.when(holds_far)
        def _():
            for d in range(1, n_seq):
                far_share(d).wait_send()
            for d in range(n_seq):
                far_pass(d).wait_send()

        @pl.when(is_helper)
        def _():
            for c in range(chunks):
                part_copy(c).wait_send()

    for c in range(chunks):
        for s in range(hops - 1):
            @pl.when(right_sends(s))
            def _():
                right_copy(c, s).wait_send()

            @pl.when(left_sends(s))
            def _():
                left_copy(c, s).wait_send()
    for d in range(1, reach + 1):
        @pl.when(has_later(d))
        def _():
            for copy in key_copies(d):
                copy.wait_send()

        @pl.when(has_earlier(d))
        def _():
            query_copy(d).wait_send()
            lse_copy(d).wait_send()
            for c in range(chunks):
                for copy in grad_copies(c, d):
                    copy.wait_send()


def place_kernel(a_in, b_in, c_in, a_out, b_out, c_out, sems):
    copies = [
        pltpu.make_async_copy(src, dst, sems.at[i])
        for i, (src, dst) in enumerate(((a_in, a_out), (b_in, b_out), (c_in, c_out)))
    ]
    for copy in copies:
        copy.start()
    for copy in copies:
        copy.wait()


def per_device(mesh, queries, keys, values, cotangent, out_weight):
    n_seq, n_tensor, n_fsdp = mesh.shape["seq"], mesh.shape["tensor"], mesh.shape["fsdp"]
    q, k, v, c = queries[0], keys[0], values[0], cotangent[0].T
    rows = q.shape[0]
    reach = min(WINDOW // rows, n_seq - 1)
    lean = is_lean(n_seq, n_tensor, n_fsdp, reach)
    heads, kv_heads = q.shape[1] // HEAD_SIZE, k.shape[1] // HEAD_SIZE
    chunks = rows // CHUNK
    bf16, f32 = jnp.bfloat16, jnp.float32
    vmem = pl.BlockSpec(memory_space=pltpu.VMEM)
    hbm = pl.BlockSpec(memory_space=pl.ANY)
    dma = pltpu.SemaphoreType.DMA
    dq, dk, dv = pl.pallas_call(
        functools.partial(kernel, n_seq, n_tensor, n_fsdp, reach),
        out_shape=[jax.ShapeDtypeStruct(x.shape, bf16) for x in (q, k, v)],
        in_specs=[vmem, vmem, vmem, hbm, hbm],
        out_specs=[vmem] * 3,
        scratch_shapes=[
            pltpu.VMEM((n_tensor * c.shape[0], rows), bf16),
            pltpu.VMEM((n_fsdp,) + out_weight.shape, bf16),
            pltpu.VMEM((reach,) + k.shape, bf16),
            pltpu.VMEM((reach,) + v.shape, bf16),
            pltpu.VMEM((reach,) + q.shape, bf16),
            pltpu.VMEM((8, rows), f32),
            pltpu.VMEM((reach, 8, rows), f32),
            pltpu.VMEM((chunks, 8, CHUNK), f32),
            pltpu.VMEM((chunks, reach, 8, CHUNK), f32),
            pltpu.VMEM(q.shape[::-1], bf16),
            pltpu.VMEM((reach,) + q.shape[::-1], bf16),
            pltpu.VMEM((reach + 1, rows, rows), f32),
            pltpu.VMEM((heads, reach + 1, rows, rows), bf16),
            pltpu.VMEM((heads, reach, rows, rows), bf16),
            pltpu.VMEM((heads, HEAD_SIZE, rows), f32),
            pltpu.VMEM((kv_heads, reach + 1, HEAD_SIZE, rows), bf16),
            pltpu.VMEM((kv_heads, reach + 1, HEAD_SIZE, rows), bf16),
            pltpu.VMEM((1, rows), f32),
            pltpu.VMEM((1, rows), f32),
            pltpu.VMEM((HEAD_SIZE, rows), f32),
            pltpu.VMEM((HEAD_SIZE, CHUNK), f32),
            pltpu.VMEM((kv_heads, rows, HEAD_SIZE), f32),
            pltpu.VMEM((kv_heads, rows, HEAD_SIZE), f32),
            pltpu.VMEM(out_weight.shape if lean else (16, 128), bf16),
            pltpu.VMEM((out_weight.shape[0], rows) if lean else (16, 128), bf16),
            pltpu.VMEM((out_weight.shape[0], rows) if lean else (16, 128), bf16),
            dma, dma,
            dma((n_fsdp,)), dma((n_fsdp,)),
            dma((chunks, n_tensor)), dma((chunks, n_tensor)),
            dma((chunks, n_tensor)), dma((chunks, n_tensor)),
            dma((3, reach + 1)), dma((3, reach + 1)),
            dma((reach + 1,)), dma((reach + 1,)),
            dma((2, chunks, reach + 1)), dma((2, chunks, reach + 1)),
            dma((n_seq,)), dma((n_seq,)), dma((n_seq,)), dma((n_seq,)), dma((chunks,)), dma((chunks,)),
        ],
        compiler_params=pltpu.CompilerParams(
            collective_id=0, has_side_effects=True, vmem_limit_bytes=56 * 2**20
        ),
        cost_estimate=pl.CostEstimate(flops=4 * 10**9, bytes_accessed=8 * 10**6, transcendentals=4 * 10**6),
    )(q, k, v, c, out_weight)
    dq, dk, dv = pl.pallas_call(
        place_kernel,
        out_shape=[jax.ShapeDtypeStruct(x.shape, bf16) for x in (q, k, v)],
        in_specs=[vmem] * 3,
        out_specs=[hbm] * 3,
        scratch_shapes=[dma((3,))],
    )(dq, dk, dv)
    return dq[None], dk[None], dv[None]


def solution(mesh):
    parts = P("fsdp", "seq", "tensor")
    return jax.shard_map(
        functools.partial(per_device, mesh),
        mesh=mesh,
        in_specs=(parts, parts, parts, parts, P("tensor", "fsdp")),
        out_specs=(parts, parts, parts),
        check_vma=False,
    )
```

```python
import functools

import jax
import jax.numpy as jnp
from jax import lax
from jax.experimental import pallas as pl
from jax.experimental.pallas import tpu as pltpu
from jax.sharding import PartitionSpec as P

HEAD_SIZE = 128
WINDOW = 1024
CHUNK = 128

score_scale = 168.0 ** (-0.5)
masked_score = -1e30
MESH = pl.DeviceIdType.MESH
NT = (((1,), (1,)), ((), ()))


def dot(a, b):
    return jnp.dot(a, b, preferred_element_type=jnp.float32)


def dot_nt(a, b):
    return lax.dot_general(a, b, NT, preferred_element_type=jnp.float32)


def is_lean(n_seq, n_tensor, n_fsdp, reach):
    return False


def kernel(
    n_seq, n_tensor, n_fsdp, reach,
    q_ref, k_ref, v_ref, c_ref, w_ref,
    dq_ref, dk_ref, dv_ref,
    c_all, w_all, k_in, v_in, q_in, lse_own, lse_in, row_own, row_in, g_own, g_in,
    s_buf, p_own, p_late, att, k_turn, v_turn, top, total, dq_acc, dk_acc, dv_acc,
    w_far, part_out, part_in,
    c_loc, w_loc, w_send, w_recv, right_send, right_recv, left_send, left_recv,
    kv_send, kv_recv, lse_send, lse_recv, g_send, g_recv,
    far_send, far_recv, pass_send, pass_recv, part_send, part_recv,
):
    rows = q_ref.shape[0]
    kv_heads = k_ref.shape[1] // HEAD_SIZE
    groups = q_ref.shape[1] // k_ref.shape[1]
    heads = kv_heads * groups
    chunks = rows // CHUNK
    features = c_ref.shape[0]
    fsdp_features = w_ref.shape[1]
    me_s, me_t, me_f = lax.axis_index("seq"), lax.axis_index("tensor"), lax.axis_index("fsdp")

    def seq_at(offset):
        return {"seq": lax.rem(me_s + offset + n_seq, n_seq)}

    def tensor_at(offset):
        return {"tensor": lax.rem(me_t + offset + n_tensor, n_tensor)}

    def fsdp_at(offset):
        return {"fsdp": lax.rem(me_f + offset + n_fsdp, n_fsdp)}

    seq_offsets = sorted({d % n_seq for r in range(1, reach + 1) for d in (r, -r)} - {0})
    tensor_offsets = sorted({1 % n_tensor, (n_tensor - 1) % n_tensor} - {0})
    peers = (
        [seq_at(d) for d in seq_offsets]
        + [tensor_at(d) for d in tensor_offsets]
        + [fsdp_at(d) for d in range(1, n_fsdp)]
    )
    barrier = pltpu.get_barrier_semaphore()
    for peer in peers:
        pl.semaphore_signal(barrier, inc=1, device_id=peer, device_id_type=MESH)
    pl.semaphore_wait(barrier, len(peers))

    def remote(src, dst, send, recv, peer):
        return pltpu.make_async_remote_copy(
            src_ref=src, dst_ref=dst, send_sem=send, recv_sem=recv,
            device_id=peer, device_id_type=MESH,
        )

    def has_earlier(d):
        return me_s >= d

    def has_later(d):
        return me_s + d < n_seq

    def block(slot):
        return pl.ds(pl.multiple_of(slot * features, 16), features)

    def right_copy(c, s):
        place = pl.ds(c * CHUNK, CHUNK)
        slot = lax.rem(me_t - s + n_tensor, n_tensor)
        there = c_all.at[block(slot), place]
        src = c_ref.at[:, place] if s == 0 else there
        return remote(src, there, right_send.at[c, s], right_recv.at[c, s], tensor_at(1))

    def left_copy(c, s):
        place = pl.ds(c * CHUNK, CHUNK)
        slot = lax.rem(me_t + s, n_tensor)
        there = c_all.at[block(slot), place]
        src = c_ref.at[:, place] if s == 0 else there
        return remote(src, there, left_send.at[c, s], left_recv.at[c, s], tensor_at(-1))

    lean = is_lean(n_seq, n_tensor, n_fsdp, reach)
    is_end = (me_t == 0) | (me_t == 3)
    is_helper = (me_t == 1) | (me_t == 2)
    far_shard = 1 - lax.div(me_t, 2)
    gives_far = is_end & (me_f == far_shard)
    holds_far = is_helper & (me_f == far_shard)
    takes_far = is_helper & (me_f != far_shard)

    def far_rows(offset):
        quarter = w_ref.shape[0] // n_seq
        piece = lax.rem(me_s - offset + n_seq, n_seq)
        return pl.ds(pl.multiple_of(piece * quarter, 16), quarter)

    def far_first():
        place = far_rows(0)
        return remote(w_ref.at[place], w_far.at[place], far_send.at[0], far_recv.at[0],
                      {"tensor": 1 + lax.div(me_t, 3)})

    def far_share(d):
        place = far_rows(0)
        return remote(w_far.at[place], w_far.at[place], far_send.at[d], far_recv.at[d], seq_at(d))

    def far_pass(d):
        place = far_rows(d)
        return remote(w_far.at[place], w_far.at[place], pass_send.at[d], pass_recv.at[d], fsdp_at(1))

    def part_copy(c):
        place = pl.ds(c * CHUNK, CHUNK)
        return remote(part_out.at[:, place], part_in.at[:, place], part_send.at[c], part_recv.at[c],
                      {"tensor": 3 * lax.div(me_t, 2)})

    def right_sends(s):
        if lean and s > 0:
            return me_t == 1
        return (me_t + 1 < n_tensor) & (me_t >= s)

    def left_sends(s):
        if lean and s > 0:
            return me_t == 2
        return (me_t >= 1) & (me_t + s < n_tensor)

    def right_lands(s):
        return me_t == 2 if lean and s > 1 else me_t >= s

    def left_lands(s):
        return me_t == 1 if lean and s > 1 else me_t + s < n_tensor

    hops = 3 if lean else n_tensor

    def w_copy(o):
        return remote(w_ref, w_all.at[me_f], w_send.at[o], w_recv.at[o], fsdp_at(o))

    def key_copies(d):
        return [
            remote(k_ref, k_in.at[d - 1], kv_send.at[0, d], kv_recv.at[0, d], seq_at(d)),
            remote(v_ref, v_in.at[d - 1], kv_send.at[1, d], kv_recv.at[1, d], seq_at(d)),
        ]

    def query_copy(d):
        return remote(q_ref, q_in.at[d - 1], kv_send.at[2, d], kv_recv.at[2, d], seq_at(-d))

    def lse_copy(d):
        return remote(lse_own, lse_in.at[d - 1], lse_send.at[d], lse_recv.at[d], seq_at(-d))

    def grad_copies(c, d):
        place = pl.ds(c * CHUNK, CHUNK)
        return [
            remote(g_own.at[:, place], g_in.at[d - 1, :, place], g_send.at[0, c, d], g_recv.at[0, c, d], seq_at(-d)),
            remote(row_own.at[c], row_in.at[c, d - 1], g_send.at[1, c, d], g_recv.at[1, c, d], seq_at(-d)),
        ]

    for c in range(chunks):
        @pl.when(right_sends(0))
        def _():
            right_copy(c, 0).start()

        @pl.when(left_sends(0))
        def _():
            left_copy(c, 0).start()

        if lean and c == 0:
            @pl.when(gives_far)
            def _():
                far_first().start()
    for o in range(1, n_fsdp):
        w_copy(o).start()
    for d in range(1, reach + 1):
        @pl.when(has_later(d))
        def _():
            for copy in key_copies(d):
                copy.start()

        @pl.when(has_earlier(d))
        def _():
            query_copy(d).start()

    def pump(c, s):
        @pl.when(right_lands(s))
        def _():
            right_copy(c, s - 1).wait_recv()

        if s < hops - 1:
            @pl.when(right_sends(s))
            def _():
                right_copy(c, s).start()

        @pl.when(left_lands(s))
        def _():
            left_copy(c, s - 1).wait_recv()

        if s < hops - 1:
            @pl.when(left_sends(s))
            def _():
                left_copy(c, s).start()

    pumped = []

    def pump_next(count):
        order = [(c, s) for s in range(1, min(3, hops)) for c in range(chunks)]
        order += [(c, s) for c in range(chunks) for s in range(3, hops)]
        for c, s in order[len(pumped) : len(pumped) + count]:
            pump(c, s)
            pumped.append((c, s))

    own_c = pltpu.make_async_copy(c_ref, c_all.at[block(me_t)], c_loc)
    own_c.start()
    own_w = pltpu.make_async_copy(w_ref, w_all.at[me_f], w_loc)
    own_w.start()

    def lanes(h):
        return slice(h * HEAD_SIZE, (h + 1) * HEAD_SIZE)

    def key_block(d):
        return k_ref if d == 0 else k_in.at[d - 1]

    def value_block(d):
        return v_ref if d == 0 else v_in.at[d - 1]

    def on_earlier(d, do):
        if d == 0:
            do()
        else:
            pl.when(has_earlier(d))(do)

    def masked(scores, d):
        shape = (rows, rows)
        if d == 0:
            j, i = lax.broadcasted_iota(jnp.int32, shape, 0), lax.broadcasted_iota(jnp.int32, shape, 1)
            return jnp.where(j <= i, scores, masked_score)
        if (d + 1) * rows - 1 >= WINDOW:
            j, i = lax.broadcasted_iota(jnp.int32, shape, 0), lax.broadcasted_iota(jnp.int32, shape, 1)
            return jnp.where(j - i > d * rows - WINDOW, scores, masked_score)
        return scores

    pump_next(1)
    lse_own[...] = jnp.zeros_like(lse_own)
    row_own[...] = jnp.zeros_like(row_own)
    for d in range(1, reach + 1):
        @pl.when(has_earlier(d))
        def _():
            for copy in key_copies(d):
                copy.wait_recv()

    for d in range(reach + 1):
        def score():
            for kv in range(kv_heads):
                k_turn[kv, d] = key_block(d)[:, lanes(kv)].T
                v_turn[kv, d] = value_block(d)[:, lanes(kv)].T
            for h in range(heads):
                scores = masked(dot_nt(key_block(d)[:, lanes(h // groups)], q_ref[:, lanes(h)]) * score_scale, d)
                s_buf[h, d] = scores
                high = jnp.max(scores, axis=0, keepdims=True)
                top[h] = high if d == 0 else jnp.maximum(top[h], high)
        on_earlier(d, score)
    pump_next(1)
    for d in range(reach + 1):
        def add():
            for h in range(heads):
                powers = jnp.exp(s_buf[h, d] - top[h])
                part = jnp.sum(powers, axis=0, keepdims=True)
                total[h] = part if d == 0 else total[h] + part
        on_earlier(d, add)
    for h in range(heads):
        lse_own[h : h + 1, :] = top[h] + jnp.log(total[h])
    for d in range(1, reach + 1):
        @pl.when(has_earlier(d))
        def _():
            lse_copy(d).start()

    for d in range(reach + 1):
        def spread():
            for h in range(heads):
                low = jnp.exp(s_buf[h, d] - lse_own[h : h + 1, :]).astype(jnp.bfloat16)
                p_own[h, d] = low
                part = dot(v_turn[h // groups, d], low)
                att[h] = part if d == 0 else att[h] + part
        on_earlier(d, spread)

    if lean:
        @pl.when(holds_far)
        def _():
            far_first().wait_recv()
            for d in range(1, n_seq):
                far_share(d).start()
            far_pass(0).start()

    own_w.wait()
    for o in range(1, n_fsdp):
        w_copy(o).wait_recv()
    pump_next(1)

    for d in range(1, reach + 1):
        @pl.when(has_later(d))
        def _():
            query_copy(d).wait_recv()
            lse_copy(d).wait_recv()

            for h in range(heads):
                scores = masked(dot_nt(k_ref[:, lanes(h // groups)], q_in[d - 1, :, lanes(h)]) * score_scale, d)
                p_late[h, d - 1] = jnp.exp(scores - lse_in[d - 1, h : h + 1, :]).astype(jnp.bfloat16)

    if lean:
        @pl.when(holds_far)
        def _():
            for d in range(1, n_seq):
                far_share(d).wait_recv()
                far_pass(d).start()

        @pl.when(takes_far)
        def _():
            for d in range(n_seq):
                far_pass(d).wait_recv()

    dk_acc[...] = jnp.zeros_like(dk_acc)
    dv_acc[...] = jnp.zeros_like(dv_acc)
    own_c.wait()

    def late_keys(c):
        place = pl.ds(c * CHUNK, CHUNK)
        for d in range(1, reach + 1):
            @pl.when(has_later(d))
            def _():
                for copy in grad_copies(c, d):
                    copy.wait_recv()

                for kv in range(kv_heads):
                    k_part, v_part = dk_acc[kv], dv_acc[kv]
                    for h in range(kv * groups, (kv + 1) * groups):
                        g = g_in[d - 1, lanes(h), place]
                        probs = p_late[h, d - 1, :, place]
                        slope = dot(v_ref[:, lanes(kv)], g) - row_in[c, d - 1, h : h + 1, :]
                        low = (probs.astype(jnp.float32) * slope).astype(jnp.bfloat16)
                        k_part += dot(low, q_in[d - 1, place, lanes(h)])
                        v_part += dot_nt(probs, g)
                    dk_acc[kv], dv_acc[kv] = k_part, v_part

    for c in range(chunks):
        place = pl.ds(c * CHUNK, CHUNK)
        if c > 0:
            late_keys(c - 1)
        while not all((c, s) in pumped for s in range(1, hops)):
            pump_next(1)
        def full_sums():
            sums = dot(w_all[0], c_all[:fsdp_features, place])
            for f in range(1, n_fsdp):
                sums += dot(w_all[f], c_all[f * fsdp_features : (f + 1) * fsdp_features, place])
            g_own[:, place] = sums.astype(jnp.bfloat16)

        def shard_features(f):
            return pl.ds(pl.multiple_of(f * fsdp_features, 16), fsdp_features)

        if lean:
            @pl.when(is_helper)
            def _():
                part = dot(w_far[...], c_all[shard_features(far_shard), place])
                part_out[:, place] = part.astype(jnp.bfloat16)
                part_copy(c).start()
                full_sums()

            @pl.when(is_end)
            def _():
                near = 1 - far_shard
                sums = dot(w_all[near], c_all[shard_features(near), place])
                part_copy(c).wait_recv()
                g_own[:, place] = (sums + part_in[:, place].astype(jnp.float32)).astype(jnp.bfloat16)
        else:
            full_sums()

        for h in range(heads):
            product = g_own[lanes(h), place].astype(jnp.float32) * att[h, :, place]
            row_own[c, h : h + 1, :] = jnp.sum(product, axis=0, keepdims=True)

        for d in range(1, reach + 1):
            @pl.when(has_earlier(d))
            def _():
                for copy in grad_copies(c, d):
                    copy.start()

        for d in range(reach + 1):
            def query_part():
                for kv in range(kv_heads):
                    for h in range(kv * groups, (kv + 1) * groups):
                        g = g_own[lanes(h), place]
                        probs = p_own[h, d, :, place]
                        slope = dot(value_block(d)[:, lanes(kv)], g) - row_own[c, h : h + 1, :]
                        low = (probs.astype(jnp.float32) * slope).astype(jnp.bfloat16)
                        part = dot(k_turn[kv, d], low)
                        if d == 0:
                            dq_acc[h] = part
                            dk_acc[kv] += dot(low, q_ref[place, lanes(h)])
                            dv_acc[kv] += dot_nt(probs, g)
                        else:
                            dq_acc[h] += part
            on_earlier(d, query_part)
        for h in range(heads):
            dq_ref[place, lanes(h)] = (dq_acc[h] * score_scale).T.astype(jnp.bfloat16)

    late_keys(chunks - 1)
    for kv in range(kv_heads):
        lane = slice(kv * HEAD_SIZE, (kv + 1) * HEAD_SIZE)
        dk_ref[:, lane] = (dk_acc[kv] * score_scale).astype(jnp.bfloat16)
        dv_ref[:, lane] = dv_acc[kv].astype(jnp.bfloat16)

    for o in range(1, n_fsdp):
        w_copy(o).wait_send()
    if lean:
        @pl.when(gives_far)
        def _():
            far_first().wait_send()

        @pl.when(holds_far)
        def _():
            for d in range(1, n_seq):
                far_share(d).wait_send()
            for d in range(n_seq):
                far_pass(d).wait_send()

        @pl.when(is_helper)
        def _():
            for c in range(chunks):
                part_copy(c).wait_send()

    for c in range(chunks):
        for s in range(hops - 1):
            @pl.when(right_sends(s))
            def _():
                right_copy(c, s).wait_send()

            @pl.when(left_sends(s))
            def _():
                left_copy(c, s).wait_send()
    for d in range(1, reach + 1):
        @pl.when(has_later(d))
        def _():
            for copy in key_copies(d):
                copy.wait_send()

        @pl.when(has_earlier(d))
        def _():
            query_copy(d).wait_send()
            lse_copy(d).wait_send()
            for c in range(chunks):
                for copy in grad_copies(c, d):
                    copy.wait_send()


def place_kernel(a_in, b_in, c_in, a_out, b_out, c_out, sems):
    copies = [
        pltpu.make_async_copy(src, dst, sems.at[i])
        for i, (src, dst) in enumerate(((a_in, a_out), (b_in, b_out), (c_in, c_out)))
    ]
    for copy in copies:
        copy.start()
    for copy in copies:
        copy.wait()


def per_device(mesh, queries, keys, values, cotangent, out_weight):
    n_seq, n_tensor, n_fsdp = mesh.shape["seq"], mesh.shape["tensor"], mesh.shape["fsdp"]
    q, k, v, c = queries[0], keys[0], values[0], cotangent[0].T
    rows = q.shape[0]
    reach = min(WINDOW // rows, n_seq - 1)
    lean = is_lean(n_seq, n_tensor, n_fsdp, reach)
    heads, kv_heads = q.shape[1] // HEAD_SIZE, k.shape[1] // HEAD_SIZE
    chunks = rows // CHUNK
    bf16, f32 = jnp.bfloat16, jnp.float32
    vmem = pl.BlockSpec(memory_space=pltpu.VMEM)
    hbm = pl.BlockSpec(memory_space=pl.ANY)
    dma = pltpu.SemaphoreType.DMA
    dq, dk, dv = pl.pallas_call(
        functools.partial(kernel, n_seq, n_tensor, n_fsdp, reach),
        out_shape=[jax.ShapeDtypeStruct(x.shape, bf16) for x in (q, k, v)],
        in_specs=[vmem, vmem, vmem, hbm, hbm],
        out_specs=[vmem] * 3,
        scratch_shapes=[
            pltpu.VMEM((n_tensor * c.shape[0], rows), bf16),
            pltpu.VMEM((n_fsdp,) + out_weight.shape, bf16),
            pltpu.VMEM((reach,) + k.shape, bf16),
            pltpu.VMEM((reach,) + v.shape, bf16),
            pltpu.VMEM((reach,) + q.shape, bf16),
            pltpu.VMEM((8, rows), f32),
            pltpu.VMEM((reach, 8, rows), f32),
            pltpu.VMEM((chunks, 8, CHUNK), f32),
            pltpu.VMEM((chunks, reach, 8, CHUNK), f32),
            pltpu.VMEM(q.shape[::-1], bf16),
            pltpu.VMEM((reach,) + q.shape[::-1], bf16),
            pltpu.VMEM((heads, reach + 1, rows, rows), f32),
            pltpu.VMEM((heads, reach + 1, rows, rows), bf16),
            pltpu.VMEM((heads, reach, rows, rows), bf16),
            pltpu.VMEM((heads, HEAD_SIZE, rows), f32),
            pltpu.VMEM((kv_heads, reach + 1, HEAD_SIZE, rows), bf16),
            pltpu.VMEM((kv_heads, reach + 1, HEAD_SIZE, rows), bf16),
            pltpu.VMEM((heads, 1, rows), f32),
            pltpu.VMEM((heads, 1, rows), f32),
            pltpu.VMEM((heads, HEAD_SIZE, CHUNK), f32),
            pltpu.VMEM((kv_heads, rows, HEAD_SIZE), f32),
            pltpu.VMEM((kv_heads, rows, HEAD_SIZE), f32),
            pltpu.VMEM(out_weight.shape if lean else (16, 128), bf16),
            pltpu.VMEM((out_weight.shape[0], rows) if lean else (16, 128), bf16),
            pltpu.VMEM((out_weight.shape[0], rows) if lean else (16, 128), bf16),
            dma, dma,
            dma((n_fsdp,)), dma((n_fsdp,)),
            dma((chunks, n_tensor)), dma((chunks, n_tensor)),
            dma((chunks, n_tensor)), dma((chunks, n_tensor)),
            dma((3, reach + 1)), dma((3, reach + 1)),
            dma((reach + 1,)), dma((reach + 1,)),
            dma((2, chunks, reach + 1)), dma((2, chunks, reach + 1)),
            dma((n_seq,)), dma((n_seq,)), dma((n_seq,)), dma((n_seq,)), dma((chunks,)), dma((chunks,)),
        ],
        compiler_params=pltpu.CompilerParams(
            collective_id=0, has_side_effects=True, vmem_limit_bytes=56 * 2**20
        ),
        cost_estimate=pl.CostEstimate(flops=4 * 10**9, bytes_accessed=8 * 10**6, transcendentals=4 * 10**6),
    )(q, k, v, c, out_weight)
    dq, dk, dv = pl.pallas_call(
        place_kernel,
        out_shape=[jax.ShapeDtypeStruct(x.shape, bf16) for x in (q, k, v)],
        in_specs=[vmem] * 3,
        out_specs=[hbm] * 3,
        scratch_shapes=[dma((3,))],
    )(dq, dk, dv)
    return dq[None], dk[None], dv[None]


def solution(mesh):
    parts = P("fsdp", "seq", "tensor")
    return jax.shard_map(
        functools.partial(per_device, mesh),
        mesh=mesh,
        in_specs=(parts, parts, parts, parts, P("tensor", "fsdp")),
        out_specs=(parts, parts, parts),
        check_vma=False,
    )
```

```python
import functools

import jax
import jax.numpy as jnp
from jax import lax
from jax.experimental import pallas as pl
from jax.experimental.pallas import tpu as pltpu
from jax.sharding import PartitionSpec as P

HEAD_SIZE = 128
WINDOW = 1024
CHUNK = 128

score_scale = 168.0 ** (-0.5)
masked_score = -1e30
MESH = pl.DeviceIdType.MESH
NT = (((1,), (1,)), ((), ()))


def dot(a, b):
    return jnp.dot(a, b, preferred_element_type=jnp.float32)


def dot_nt(a, b):
    return lax.dot_general(a, b, NT, preferred_element_type=jnp.float32)


def is_lean(n_seq, n_tensor, n_fsdp, reach):
    return False


def kernel(
    n_seq, n_tensor, n_fsdp, reach,
    q_ref, k_ref, v_ref, c_ref, w_ref,
    dq_ref, dk_ref, dv_ref,
    c_all, w_all, k_in, v_in, q_in, lse_own, lse_in, row_own, row_in, g_own, g_in,
    s_buf, p_own, p_late, att, k_turn, v_turn, top, total, dq_acc, dk_acc, dv_acc,
    w_far, part_out, part_in,
    c_loc, w_loc, w_send, w_recv, right_send, right_recv, left_send, left_recv,
    kv_send, kv_recv, lse_send, lse_recv, g_send, g_recv,
    far_send, far_recv, pass_send, pass_recv, part_send, part_recv,
):
    rows = q_ref.shape[0]
    kv_heads = k_ref.shape[1] // HEAD_SIZE
    groups = q_ref.shape[1] // k_ref.shape[1]
    heads = kv_heads * groups
    chunks = rows // CHUNK
    features = c_ref.shape[0]
    fsdp_features = w_ref.shape[1]
    me_s, me_t, me_f = lax.axis_index("seq"), lax.axis_index("tensor"), lax.axis_index("fsdp")

    def seq_at(offset):
        return {"seq": lax.rem(me_s + offset + n_seq, n_seq)}

    def tensor_at(offset):
        return {"tensor": lax.rem(me_t + offset + n_tensor, n_tensor)}

    def fsdp_at(offset):
        return {"fsdp": lax.rem(me_f + offset + n_fsdp, n_fsdp)}

    seq_offsets = sorted({d % n_seq for r in range(1, reach + 1) for d in (r, -r)} - {0})
    tensor_offsets = sorted({1 % n_tensor, (n_tensor - 1) % n_tensor} - {0})
    peers = (
        [seq_at(d) for d in seq_offsets]
        + [tensor_at(d) for d in tensor_offsets]
        + [fsdp_at(d) for d in range(1, n_fsdp)]
    )
    barrier = pltpu.get_barrier_semaphore()
    for peer in peers:
        pl.semaphore_signal(barrier, inc=1, device_id=peer, device_id_type=MESH)
    pl.semaphore_wait(barrier, len(peers))

    def remote(src, dst, send, recv, peer):
        return pltpu.make_async_remote_copy(
            src_ref=src, dst_ref=dst, send_sem=send, recv_sem=recv,
            device_id=peer, device_id_type=MESH,
        )

    def has_earlier(d):
        return me_s >= d

    def has_later(d):
        return me_s + d < n_seq

    def block(slot):
        return pl.ds(pl.multiple_of(slot * features, 16), features)

    def right_copy(c, s):
        place = pl.ds(c * CHUNK, CHUNK)
        slot = lax.rem(me_t - s + n_tensor, n_tensor)
        there = c_all.at[block(slot), place]
        src = c_ref.at[:, place] if s == 0 else there
        return remote(src, there, right_send.at[c, s], right_recv.at[c, s], tensor_at(1))

    def left_copy(c, s):
        place = pl.ds(c * CHUNK, CHUNK)
        slot = lax.rem(me_t + s, n_tensor)
        there = c_all.at[block(slot), place]
        src = c_ref.at[:, place] if s == 0 else there
        return remote(src, there, left_send.at[c, s], left_recv.at[c, s], tensor_at(-1))

    lean = is_lean(n_seq, n_tensor, n_fsdp, reach)
    is_end = (me_t == 0) | (me_t == 3)
    is_helper = (me_t == 1) | (me_t == 2)
    far_shard = 1 - lax.div(me_t, 2)
    gives_far = is_end & (me_f == far_shard)
    holds_far = is_helper & (me_f == far_shard)
    takes_far = is_helper & (me_f != far_shard)

    def far_rows(offset):
        quarter = w_ref.shape[0] // n_seq
        piece = lax.rem(me_s - offset + n_seq, n_seq)
        return pl.ds(pl.multiple_of(piece * quarter, 16), quarter)

    def far_first():
        place = far_rows(0)
        return remote(w_ref.at[place], w_far.at[place], far_send.at[0], far_recv.at[0],
                      {"tensor": 1 + lax.div(me_t, 3)})

    def far_share(d):
        place = far_rows(0)
        return remote(w_far.at[place], w_far.at[place], far_send.at[d], far_recv.at[d], seq_at(d))

    def far_pass(d):
        place = far_rows(d)
        return remote(w_far.at[place], w_far.at[place], pass_send.at[d], pass_recv.at[d], fsdp_at(1))

    def part_copy(c):
        place = pl.ds(c * CHUNK, CHUNK)
        return remote(part_out.at[:, place], part_in.at[:, place], part_send.at[c], part_recv.at[c],
                      {"tensor": 3 * lax.div(me_t, 2)})

    def right_sends(s):
        if lean and s > 0:
            return me_t == 1
        return (me_t + 1 < n_tensor) & (me_t >= s)

    def left_sends(s):
        if lean and s > 0:
            return me_t == 2
        return (me_t >= 1) & (me_t + s < n_tensor)

    def right_lands(s):
        return me_t == 2 if lean and s > 1 else me_t >= s

    def left_lands(s):
        return me_t == 1 if lean and s > 1 else me_t + s < n_tensor

    hops = 3 if lean else n_tensor

    def w_copy(o):
        return remote(w_ref, w_all.at[me_f], w_send.at[o], w_recv.at[o], fsdp_at(o))

    def key_copies(d):
        return [
            remote(k_ref, k_in.at[d - 1], kv_send.at[0, d], kv_recv.at[0, d], seq_at(d)),
            remote(v_ref, v_in.at[d - 1], kv_send.at[1, d], kv_recv.at[1, d], seq_at(d)),
        ]

    def query_copy(d):
        return remote(q_ref, q_in.at[d - 1], kv_send.at[2, d], kv_recv.at[2, d], seq_at(-d))

    def lse_copy(d):
        return remote(lse_own, lse_in.at[d - 1], lse_send.at[d], lse_recv.at[d], seq_at(-d))

    def grad_copies(c, d):
        place = pl.ds(c * CHUNK, CHUNK)
        return [
            remote(g_own.at[:, place], g_in.at[d - 1, :, place], g_send.at[0, c, d], g_recv.at[0, c, d], seq_at(-d)),
            remote(row_own.at[c], row_in.at[c, d - 1], g_send.at[1, c, d], g_recv.at[1, c, d], seq_at(-d)),
        ]

    for c in range(chunks):
        @pl.when(right_sends(0))
        def _():
            right_copy(c, 0).start()

        @pl.when(left_sends(0))
        def _():
            left_copy(c, 0).start()

        if lean and c == 0:
            @pl.when(gives_far)
            def _():
                far_first().start()
    for o in range(1, n_fsdp):
        w_copy(o).start()
    for d in range(1, reach + 1):
        @pl.when(has_later(d))
        def _():
            for copy in key_copies(d):
                copy.start()

        @pl.when(has_earlier(d))
        def _():
            query_copy(d).start()

    def pump(c, s):
        @pl.when(right_lands(s))
        def _():
            right_copy(c, s - 1).wait_recv()

        if s < hops - 1:
            @pl.when(right_sends(s))
            def _():
                right_copy(c, s).start()

        @pl.when(left_lands(s))
        def _():
            left_copy(c, s - 1).wait_recv()

        if s < hops - 1:
            @pl.when(left_sends(s))
            def _():
                left_copy(c, s).start()

    pumped = []

    def pump_next(count):
        order = [(c, s) for s in range(1, min(3, hops)) for c in range(chunks)]
        order += [(c, s) for c in range(chunks) for s in range(3, hops)]
        for c, s in order[len(pumped) : len(pumped) + count]:
            pump(c, s)
            pumped.append((c, s))

    own_c = pltpu.make_async_copy(c_ref, c_all.at[block(me_t)], c_loc)
    own_c.start()
    own_w = pltpu.make_async_copy(w_ref, w_all.at[me_f], w_loc)
    own_w.start()

    def lanes(h):
        return slice(h * HEAD_SIZE, (h + 1) * HEAD_SIZE)

    def key_block(d):
        return k_ref if d == 0 else k_in.at[d - 1]

    def value_block(d):
        return v_ref if d == 0 else v_in.at[d - 1]

    def on_earlier(d, do):
        if d == 0:
            do()
        else:
            pl.when(has_earlier(d))(do)

    def masked(scores, d):
        shape = (rows, rows)
        if d == 0:
            j, i = lax.broadcasted_iota(jnp.int32, shape, 0), lax.broadcasted_iota(jnp.int32, shape, 1)
            return jnp.where(j <= i, scores, masked_score)
        if (d + 1) * rows - 1 >= WINDOW:
            j, i = lax.broadcasted_iota(jnp.int32, shape, 0), lax.broadcasted_iota(jnp.int32, shape, 1)
            return jnp.where(j - i > d * rows - WINDOW, scores, masked_score)
        return scores

    pump_next(chunks)
    lse_own[...] = jnp.zeros_like(lse_own)
    row_own[...] = jnp.zeros_like(row_own)
    for d in range(1, reach + 1):
        @pl.when(has_earlier(d))
        def _():
            for copy in key_copies(d):
                copy.wait_recv()

    for d in range(reach + 1):
        def score():
            for kv in range(kv_heads):
                k_turn[kv, d] = key_block(d)[:, lanes(kv)].T
                v_turn[kv, d] = value_block(d)[:, lanes(kv)].T
            for h in range(heads):
                scores = masked(dot_nt(key_block(d)[:, lanes(h // groups)], q_ref[:, lanes(h)]) * score_scale, d)
                s_buf[h, d] = scores
                high = jnp.max(scores, axis=0, keepdims=True)
                top[h] = high if d == 0 else jnp.maximum(top[h], high)
        on_earlier(d, score)
    for d in range(reach + 1):
        def add():
            for h in range(heads):
                powers = jnp.exp(s_buf[h, d] - top[h])
                part = jnp.sum(powers, axis=0, keepdims=True)
                total[h] = part if d == 0 else total[h] + part
        on_earlier(d, add)
    for h in range(heads):
        lse_own[h : h + 1, :] = top[h] + jnp.log(total[h])
    for d in range(1, reach + 1):
        @pl.when(has_earlier(d))
        def _():
            lse_copy(d).start()

    for d in range(reach + 1):
        def spread():
            for h in range(heads):
                low = jnp.exp(s_buf[h, d] - lse_own[h : h + 1, :]).astype(jnp.bfloat16)
                p_own[h, d] = low
                part = dot(v_turn[h // groups, d], low)
                att[h] = part if d == 0 else att[h] + part
        on_earlier(d, spread)

    if lean:
        @pl.when(holds_far)
        def _():
            far_first().wait_recv()
            for d in range(1, n_seq):
                far_share(d).start()
            far_pass(0).start()

    own_w.wait()
    for o in range(1, n_fsdp):
        w_copy(o).wait_recv()
    pump_next(1)

    for d in range(1, reach + 1):
        @pl.when(has_later(d))
        def _():
            query_copy(d).wait_recv()
            lse_copy(d).wait_recv()

            for h in range(heads):
                scores = masked(dot_nt(k_ref[:, lanes(h // groups)], q_in[d - 1, :, lanes(h)]) * score_scale, d)
                p_late[h, d - 1] = jnp.exp(scores - lse_in[d - 1, h : h + 1, :]).astype(jnp.bfloat16)

    if lean:
        @pl.when(holds_far)
        def _():
            for d in range(1, n_seq):
                far_share(d).wait_recv()
                far_pass(d).start()

        @pl.when(takes_far)
        def _():
            for d in range(n_seq):
                far_pass(d).wait_recv()

    pump_next(1)
    dk_acc[...] = jnp.zeros_like(dk_acc)
    dv_acc[...] = jnp.zeros_like(dv_acc)
    own_c.wait()

    def late_keys(c):
        place = pl.ds(c * CHUNK, CHUNK)
        for d in range(1, reach + 1):
            @pl.when(has_later(d))
            def _():
                for copy in grad_copies(c, d):
                    copy.wait_recv()

                for kv in range(kv_heads):
                    k_part, v_part = dk_acc[kv], dv_acc[kv]
                    for h in range(kv * groups, (kv + 1) * groups):
                        g = g_in[d - 1, lanes(h), place]
                        probs = p_late[h, d - 1, :, place]
                        slope = dot(v_ref[:, lanes(kv)], g) - row_in[c, d - 1, h : h + 1, :]
                        low = (probs.astype(jnp.float32) * slope).astype(jnp.bfloat16)
                        k_part += dot(low, q_in[d - 1, place, lanes(h)])
                        v_part += dot_nt(probs, g)
                    dk_acc[kv], dv_acc[kv] = k_part, v_part

    for c in range(chunks):
        place = pl.ds(c * CHUNK, CHUNK)
        if c > 0:
            late_keys(c - 1)
        while not all((c, s) in pumped for s in range(1, hops)):
            pump_next(1)
        def full_sums():
            sums = dot(w_all[0], c_all[:fsdp_features, place])
            for f in range(1, n_fsdp):
                sums += dot(w_all[f], c_all[f * fsdp_features : (f + 1) * fsdp_features, place])
            g_own[:, place] = sums.astype(jnp.bfloat16)

        def shard_features(f):
            return pl.ds(pl.multiple_of(f * fsdp_features, 16), fsdp_features)

        if lean:
            @pl.when(is_helper)
            def _():
                part = dot(w_far[...], c_all[shard_features(far_shard), place])
                part_out[:, place] = part.astype(jnp.bfloat16)
                part_copy(c).start()
                full_sums()

            @pl.when(is_end)
            def _():
                near = 1 - far_shard
                sums = dot(w_all[near], c_all[shard_features(near), place])
                part_copy(c).wait_recv()
                g_own[:, place] = (sums + part_in[:, place].astype(jnp.float32)).astype(jnp.bfloat16)
        else:
            full_sums()

        for h in range(heads):
            product = g_own[lanes(h), place].astype(jnp.float32) * att[h, :, place]
            row_own[c, h : h + 1, :] = jnp.sum(product, axis=0, keepdims=True)

        for d in range(1, reach + 1):
            @pl.when(has_earlier(d))
            def _():
                for copy in grad_copies(c, d):
                    copy.start()

        for d in range(reach + 1):
            def query_part():
                for kv in range(kv_heads):
                    for h in range(kv * groups, (kv + 1) * groups):
                        g = g_own[lanes(h), place]
                        probs = p_own[h, d, :, place]
                        slope = dot(value_block(d)[:, lanes(kv)], g) - row_own[c, h : h + 1, :]
                        low = (probs.astype(jnp.float32) * slope).astype(jnp.bfloat16)
                        part = dot(k_turn[kv, d], low)
                        if d == 0:
                            dq_acc[h] = part
                            dk_acc[kv] += dot(low, q_ref[place, lanes(h)])
                            dv_acc[kv] += dot_nt(probs, g)
                        else:
                            dq_acc[h] += part
            on_earlier(d, query_part)
        for h in range(heads):
            dq_ref[place, lanes(h)] = (dq_acc[h] * score_scale).T.astype(jnp.bfloat16)

    late_keys(chunks - 1)
    for kv in range(kv_heads):
        lane = slice(kv * HEAD_SIZE, (kv + 1) * HEAD_SIZE)
        dk_ref[:, lane] = (dk_acc[kv] * score_scale).astype(jnp.bfloat16)
        dv_ref[:, lane] = dv_acc[kv].astype(jnp.bfloat16)

    for o in range(1, n_fsdp):
        w_copy(o).wait_send()
    if lean:
        @pl.when(gives_far)
        def _():
            far_first().wait_send()

        @pl.when(holds_far)
        def _():
            for d in range(1, n_seq):
                far_share(d).wait_send()
            for d in range(n_seq):
                far_pass(d).wait_send()

        @pl.when(is_helper)
        def _():
            for c in range(chunks):
                part_copy(c).wait_send()

    for c in range(chunks):
        for s in range(hops - 1):
            @pl.when(right_sends(s))
            def _():
                right_copy(c, s).wait_send()

            @pl.when(left_sends(s))
            def _():
                left_copy(c, s).wait_send()
    for d in range(1, reach + 1):
        @pl.when(has_later(d))
        def _():
            for copy in key_copies(d):
                copy.wait_send()

        @pl.when(has_earlier(d))
        def _():
            query_copy(d).wait_send()
            lse_copy(d).wait_send()
            for c in range(chunks):
                for copy in grad_copies(c, d):
                    copy.wait_send()


def place_kernel(a_in, b_in, c_in, a_out, b_out, c_out, sems):
    copies = [
        pltpu.make_async_copy(src, dst, sems.at[i])
        for i, (src, dst) in enumerate(((a_in, a_out), (b_in, b_out), (c_in, c_out)))
    ]
    for copy in copies:
        copy.start()
    for copy in copies:
        copy.wait()


def per_device(mesh, queries, keys, values, cotangent, out_weight):
    n_seq, n_tensor, n_fsdp = mesh.shape["seq"], mesh.shape["tensor"], mesh.shape["fsdp"]
    q, k, v, c = queries[0], keys[0], values[0], cotangent[0].T
    rows = q.shape[0]
    reach = min(WINDOW // rows, n_seq - 1)
    lean = is_lean(n_seq, n_tensor, n_fsdp, reach)
    heads, kv_heads = q.shape[1] // HEAD_SIZE, k.shape[1] // HEAD_SIZE
    chunks = rows // CHUNK
    bf16, f32 = jnp.bfloat16, jnp.float32
    vmem = pl.BlockSpec(memory_space=pltpu.VMEM)
    hbm = pl.BlockSpec(memory_space=pl.ANY)
    dma = pltpu.SemaphoreType.DMA
    dq, dk, dv = pl.pallas_call(
        functools.partial(kernel, n_seq, n_tensor, n_fsdp, reach),
        out_shape=[jax.ShapeDtypeStruct(x.shape, bf16) for x in (q, k, v)],
        in_specs=[vmem, vmem, vmem, hbm, hbm],
        out_specs=[vmem] * 3,
        scratch_shapes=[
            pltpu.VMEM((n_tensor * c.shape[0], rows), bf16),
            pltpu.VMEM((n_fsdp,) + out_weight.shape, bf16),
            pltpu.VMEM((reach,) + k.shape, bf16),
            pltpu.VMEM((reach,) + v.shape, bf16),
            pltpu.VMEM((reach,) + q.shape, bf16),
            pltpu.VMEM((8, rows), f32),
            pltpu.VMEM((reach, 8, rows), f32),
            pltpu.VMEM((chunks, 8, CHUNK), f32),
            pltpu.VMEM((chunks, reach, 8, CHUNK), f32),
            pltpu.VMEM(q.shape[::-1], bf16),
            pltpu.VMEM((reach,) + q.shape[::-1], bf16),
            pltpu.VMEM((heads, reach + 1, rows, rows), f32),
            pltpu.VMEM((heads, reach + 1, rows, rows), bf16),
            pltpu.VMEM((heads, reach, rows, rows), bf16),
            pltpu.VMEM((heads, HEAD_SIZE, rows), f32),
            pltpu.VMEM((kv_heads, reach + 1, HEAD_SIZE, rows), bf16),
            pltpu.VMEM((kv_heads, reach + 1, HEAD_SIZE, rows), bf16),
            pltpu.VMEM((heads, 1, rows), f32),
            pltpu.VMEM((heads, 1, rows), f32),
            pltpu.VMEM((heads, HEAD_SIZE, CHUNK), f32),
            pltpu.VMEM((kv_heads, rows, HEAD_SIZE), f32),
            pltpu.VMEM((kv_heads, rows, HEAD_SIZE), f32),
            pltpu.VMEM(out_weight.shape if lean else (16, 128), bf16),
            pltpu.VMEM((out_weight.shape[0], rows) if lean else (16, 128), bf16),
            pltpu.VMEM((out_weight.shape[0], rows) if lean else (16, 128), bf16),
            dma, dma,
            dma((n_fsdp,)), dma((n_fsdp,)),
            dma((chunks, n_tensor)), dma((chunks, n_tensor)),
            dma((chunks, n_tensor)), dma((chunks, n_tensor)),
            dma((3, reach + 1)), dma((3, reach + 1)),
            dma((reach + 1,)), dma((reach + 1,)),
            dma((2, chunks, reach + 1)), dma((2, chunks, reach + 1)),
            dma((n_seq,)), dma((n_seq,)), dma((n_seq,)), dma((n_seq,)), dma((chunks,)), dma((chunks,)),
        ],
        compiler_params=pltpu.CompilerParams(
            collective_id=0, has_side_effects=True, vmem_limit_bytes=56 * 2**20
        ),
        cost_estimate=pl.CostEstimate(flops=4 * 10**9, bytes_accessed=8 * 10**6, transcendentals=4 * 10**6),
    )(q, k, v, c, out_weight)
    dq, dk, dv = pl.pallas_call(
        place_kernel,
        out_shape=[jax.ShapeDtypeStruct(x.shape, bf16) for x in (q, k, v)],
        in_specs=[vmem] * 3,
        out_specs=[hbm] * 3,
        scratch_shapes=[dma((3,))],
    )(dq, dk, dv)
    return dq[None], dk[None], dv[None]


def solution(mesh):
    parts = P("fsdp", "seq", "tensor")
    return jax.shard_map(
        functools.partial(per_device, mesh),
        mesh=mesh,
        in_specs=(parts, parts, parts, parts, P("tensor", "fsdp")),
        out_specs=(parts, parts, parts),
        check_vma=False,
    )
```

```python
import functools

import jax
import jax.numpy as jnp
from jax import lax
from jax.experimental import pallas as pl
from jax.experimental.pallas import tpu as pltpu
from jax.sharding import PartitionSpec as P

HEAD_SIZE = 128
WINDOW = 1024
CHUNK = 128

score_scale = 168.0 ** (-0.5)
masked_score = -1e30
MESH = pl.DeviceIdType.MESH
NT = (((1,), (1,)), ((), ()))


def dot(a, b):
    return jnp.dot(a, b, preferred_element_type=jnp.float32)


def dot_nt(a, b):
    return lax.dot_general(a, b, NT, preferred_element_type=jnp.float32)


def is_lean(n_seq, n_tensor, n_fsdp, reach):
    return n_tensor == 4 and n_fsdp == 2 and n_seq > 1 and reach == n_seq - 1


def kernel(
    n_seq, n_tensor, n_fsdp, reach,
    q_ref, k_ref, v_ref, c_ref, w_ref,
    dq_ref, dk_ref, dv_ref,
    c_all, w_all, k_in, v_in, q_in, lse_own, lse_in, row_own, row_in, g_own, g_in,
    s_buf, p_own, p_late, att, k_turn, v_turn, top, total, dq_acc, dk_acc, dv_acc,
    w_far, part_out, part_in,
    c_loc, w_loc, w_send, w_recv, right_send, right_recv, left_send, left_recv,
    kv_send, kv_recv, lse_send, lse_recv, g_send, g_recv,
    far_send, far_recv, pass_send, pass_recv, part_send, part_recv,
):
    rows = q_ref.shape[0]
    kv_heads = k_ref.shape[1] // HEAD_SIZE
    groups = q_ref.shape[1] // k_ref.shape[1]
    heads = kv_heads * groups
    chunks = rows // CHUNK
    features = c_ref.shape[0]
    fsdp_features = w_ref.shape[1]
    me_s, me_t, me_f = lax.axis_index("seq"), lax.axis_index("tensor"), lax.axis_index("fsdp")

    def seq_at(offset):
        return {"seq": lax.rem(me_s + offset + n_seq, n_seq)}

    def tensor_at(offset):
        return {"tensor": lax.rem(me_t + offset + n_tensor, n_tensor)}

    def fsdp_at(offset):
        return {"fsdp": lax.rem(me_f + offset + n_fsdp, n_fsdp)}

    seq_offsets = sorted({d % n_seq for r in range(1, reach + 1) for d in (r, -r)} - {0})
    tensor_offsets = sorted({1 % n_tensor, (n_tensor - 1) % n_tensor} - {0})
    peers = (
        [seq_at(d) for d in seq_offsets]
        + [tensor_at(d) for d in tensor_offsets]
        + [fsdp_at(d) for d in range(1, n_fsdp)]
    )
    barrier = pltpu.get_barrier_semaphore()
    for peer in peers:
        pl.semaphore_signal(barrier, inc=1, device_id=peer, device_id_type=MESH)
    pl.semaphore_wait(barrier, len(peers))

    def remote(src, dst, send, recv, peer):
        return pltpu.make_async_remote_copy(
            src_ref=src, dst_ref=dst, send_sem=send, recv_sem=recv,
            device_id=peer, device_id_type=MESH,
        )

    def has_earlier(d):
        return me_s >= d

    def has_later(d):
        return me_s + d < n_seq

    def block(slot):
        return pl.ds(pl.multiple_of(slot * features, 16), features)

    def right_copy(c, s):
        place = pl.ds(c * CHUNK, CHUNK)
        slot = lax.rem(me_t - s + n_tensor, n_tensor)
        there = c_all.at[block(slot), place]
        src = c_ref.at[:, place] if s == 0 else there
        return remote(src, there, right_send.at[c, s], right_recv.at[c, s], tensor_at(1))

    def left_copy(c, s):
        place = pl.ds(c * CHUNK, CHUNK)
        slot = lax.rem(me_t + s, n_tensor)
        there = c_all.at[block(slot), place]
        src = c_ref.at[:, place] if s == 0 else there
        return remote(src, there, left_send.at[c, s], left_recv.at[c, s], tensor_at(-1))

    lean = is_lean(n_seq, n_tensor, n_fsdp, reach)
    is_end = (me_t == 0) | (me_t == 3)
    is_helper = (me_t == 1) | (me_t == 2)
    far_shard = 1 - lax.div(me_t, 2)
    gives_far = is_end & (me_f == far_shard)
    holds_far = is_helper & (me_f == far_shard)
    takes_far = is_helper & (me_f != far_shard)

    def far_rows(offset):
        quarter = w_ref.shape[0] // n_seq
        piece = lax.rem(me_s - offset + n_seq, n_seq)
        return pl.ds(pl.multiple_of(piece * quarter, 16), quarter)

    def far_first():
        place = far_rows(0)
        return remote(w_ref.at[place], w_far.at[place], far_send.at[0], far_recv.at[0],
                      {"tensor": 1 + lax.div(me_t, 3)})

    def far_share(d):
        place = far_rows(0)
        return remote(w_far.at[place], w_far.at[place], far_send.at[d], far_recv.at[d], seq_at(d))

    def far_pass(d):
        place = far_rows(d)
        return remote(w_far.at[place], w_far.at[place], pass_send.at[d], pass_recv.at[d], fsdp_at(1))

    def part_copy(c):
        place = pl.ds(c * CHUNK, CHUNK)
        return remote(part_out.at[:, place], part_in.at[:, place], part_send.at[c], part_recv.at[c],
                      {"tensor": 3 * lax.div(me_t, 2)})

    def right_sends(s):
        if lean and s > 0:
            return me_t == 1
        return (me_t + 1 < n_tensor) & (me_t >= s)

    def left_sends(s):
        if lean and s > 0:
            return me_t == 2
        return (me_t >= 1) & (me_t + s < n_tensor)

    def right_lands(s):
        return me_t == 2 if lean and s > 1 else me_t >= s

    def left_lands(s):
        return me_t == 1 if lean and s > 1 else me_t + s < n_tensor

    hops = 3 if lean else n_tensor

    def w_copy(o):
        return remote(w_ref, w_all.at[me_f], w_send.at[o], w_recv.at[o], fsdp_at(o))

    def key_copies(d):
        return [
            remote(k_ref, k_in.at[d - 1], kv_send.at[0, d], kv_recv.at[0, d], seq_at(d)),
            remote(v_ref, v_in.at[d - 1], kv_send.at[1, d], kv_recv.at[1, d], seq_at(d)),
        ]

    def query_copy(d):
        return remote(q_ref, q_in.at[d - 1], kv_send.at[2, d], kv_recv.at[2, d], seq_at(-d))

    def lse_copy(d):
        return remote(lse_own, lse_in.at[d - 1], lse_send.at[d], lse_recv.at[d], seq_at(-d))

    def grad_copies(c, d):
        place = pl.ds(c * CHUNK, CHUNK)
        return [
            remote(g_own.at[:, place], g_in.at[d - 1, :, place], g_send.at[0, c, d], g_recv.at[0, c, d], seq_at(-d)),
            remote(row_own.at[c], row_in.at[c, d - 1], g_send.at[1, c, d], g_recv.at[1, c, d], seq_at(-d)),
        ]

    if lean:
        @pl.when(gives_far)
        def _():
            far_first().start()

    for c in range(chunks):
        @pl.when(right_sends(0))
        def _():
            right_copy(c, 0).start()

        @pl.when(left_sends(0))
        def _():
            left_copy(c, 0).start()
    for o in range(1, n_fsdp):
        w_copy(o).start()
    for d in range(1, reach + 1):
        @pl.when(has_later(d))
        def _():
            for copy in key_copies(d):
                copy.start()

        @pl.when(has_earlier(d))
        def _():
            query_copy(d).start()

    def pump(c, s):
        @pl.when(right_lands(s))
        def _():
            right_copy(c, s - 1).wait_recv()

        if s < hops - 1:
            @pl.when(right_sends(s))
            def _():
                right_copy(c, s).start()

        @pl.when(left_lands(s))
        def _():
            left_copy(c, s - 1).wait_recv()

        if s < hops - 1:
            @pl.when(left_sends(s))
            def _():
                left_copy(c, s).start()

    pumped = []

    def pump_next(count):
        order = [(c, s) for s in range(1, min(3, hops)) for c in range(chunks)]
        order += [(c, s) for c in range(chunks) for s in range(3, hops)]
        for c, s in order[len(pumped) : len(pumped) + count]:
            pump(c, s)
            pumped.append((c, s))

    own_c = pltpu.make_async_copy(c_ref, c_all.at[block(me_t)], c_loc)
    own_c.start()
    own_w = pltpu.make_async_copy(w_ref, w_all.at[me_f], w_loc)
    own_w.start()

    def lanes(h):
        return slice(h * HEAD_SIZE, (h + 1) * HEAD_SIZE)

    def key_block(d):
        return k_ref if d == 0 else k_in.at[d - 1]

    def value_block(d):
        return v_ref if d == 0 else v_in.at[d - 1]

    def on_earlier(d, do):
        if d == 0:
            do()
        else:
            pl.when(has_earlier(d))(do)

    def masked(scores, d):
        shape = (rows, rows)
        if d == 0:
            j, i = lax.broadcasted_iota(jnp.int32, shape, 0), lax.broadcasted_iota(jnp.int32, shape, 1)
            return jnp.where(j <= i, scores, masked_score)
        if (d + 1) * rows - 1 >= WINDOW:
            j, i = lax.broadcasted_iota(jnp.int32, shape, 0), lax.broadcasted_iota(jnp.int32, shape, 1)
            return jnp.where(j - i > d * rows - WINDOW, scores, masked_score)
        return scores

    if lean:
        @pl.when(holds_far)
        def _():
            far_first().wait_recv()
            for d in range(1, n_seq):
                far_share(d).start()
            far_pass(0).start()

    pump_next(chunks)
    lse_own[...] = jnp.zeros_like(lse_own)
    row_own[...] = jnp.zeros_like(row_own)
    for d in range(1, reach + 1):
        @pl.when(has_earlier(d))
        def _():
            for copy in key_copies(d):
                copy.wait_recv()

    for d in range(reach + 1):
        def score():
            for kv in range(kv_heads):
                k_turn[kv, d] = key_block(d)[:, lanes(kv)].T
                v_turn[kv, d] = value_block(d)[:, lanes(kv)].T
            for h in range(heads):
                scores = masked(dot_nt(key_block(d)[:, lanes(h // groups)], q_ref[:, lanes(h)]) * score_scale, d)
                s_buf[h, d] = scores
                high = jnp.max(scores, axis=0, keepdims=True)
                top[h] = high if d == 0 else jnp.maximum(top[h], high)
        on_earlier(d, score)
    for d in range(reach + 1):
        def add():
            for h in range(heads):
                powers = jnp.exp(s_buf[h, d] - top[h])
                part = jnp.sum(powers, axis=0, keepdims=True)
                total[h] = part if d == 0 else total[h] + part
        on_earlier(d, add)
    for h in range(heads):
        lse_own[h : h + 1, :] = top[h] + jnp.log(total[h])
    for d in range(1, reach + 1):
        @pl.when(has_earlier(d))
        def _():
            lse_copy(d).start()

    if lean:
        @pl.when(holds_far)
        def _():
            for d in range(1, n_seq):
                far_share(d).wait_recv()
                far_pass(d).start()

    for d in range(reach + 1):
        def spread():
            for h in range(heads):
                low = jnp.exp(s_buf[h, d] - lse_own[h : h + 1, :]).astype(jnp.bfloat16)
                p_own[h, d] = low
                part = dot(v_turn[h // groups, d], low)
                att[h] = part if d == 0 else att[h] + part
        on_earlier(d, spread)

    own_w.wait()
    for o in range(1, n_fsdp):
        w_copy(o).wait_recv()
    pump_next(1)

    for d in range(1, reach + 1):
        @pl.when(has_later(d))
        def _():
            query_copy(d).wait_recv()
            lse_copy(d).wait_recv()

            for h in range(heads):
                scores = masked(dot_nt(k_ref[:, lanes(h // groups)], q_in[d - 1, :, lanes(h)]) * score_scale, d)
                p_late[h, d - 1] = jnp.exp(scores - lse_in[d - 1, h : h + 1, :]).astype(jnp.bfloat16)

    if lean:
        @pl.when(takes_far)
        def _():
            for d in range(n_seq):
                far_pass(d).wait_recv()

    if not lean:
        pump_next(1)
    dk_acc[...] = jnp.zeros_like(dk_acc)
    dv_acc[...] = jnp.zeros_like(dv_acc)
    own_c.wait()

    def late_keys(c):
        place = pl.ds(c * CHUNK, CHUNK)
        for d in range(1, reach + 1):
            @pl.when(has_later(d))
            def _():
                for copy in grad_copies(c, d):
                    copy.wait_recv()

                for kv in range(kv_heads):
                    k_part, v_part = dk_acc[kv], dv_acc[kv]
                    for h in range(kv * groups, (kv + 1) * groups):
                        g = g_in[d - 1, lanes(h), place]
                        probs = p_late[h, d - 1, :, place]
                        slope = dot(v_ref[:, lanes(kv)], g) - row_in[c, d - 1, h : h + 1, :]
                        low = (probs.astype(jnp.float32) * slope).astype(jnp.bfloat16)
                        k_part += dot(low, q_in[d - 1, place, lanes(h)])
                        v_part += dot_nt(probs, g)
                    dk_acc[kv], dv_acc[kv] = k_part, v_part

    for c in range(chunks):
        place = pl.ds(c * CHUNK, CHUNK)
        if c > 0:
            late_keys(c - 1)
        while not all((c, s) in pumped for s in range(1, hops)):
            pump_next(1)
        def full_sums():
            sums = dot(w_all[0], c_all[:fsdp_features, place])
            for f in range(1, n_fsdp):
                sums += dot(w_all[f], c_all[f * fsdp_features : (f + 1) * fsdp_features, place])
            g_own[:, place] = sums.astype(jnp.bfloat16)

        def shard_features(f):
            return pl.ds(pl.multiple_of(f * fsdp_features, 16), fsdp_features)

        if lean:
            @pl.when(is_helper)
            def _():
                part = dot(w_far[...], c_all[shard_features(far_shard), place])
                part_out[:, place] = part.astype(jnp.bfloat16)
                part_copy(c).start()
                full_sums()

            @pl.when(is_end)
            def _():
                near = 1 - far_shard
                sums = dot(w_all[near], c_all[shard_features(near), place])
                part_copy(c).wait_recv()
                g_own[:, place] = (sums + part_in[:, place].astype(jnp.float32)).astype(jnp.bfloat16)
        else:
            full_sums()

        for h in range(heads):
            product = g_own[lanes(h), place].astype(jnp.float32) * att[h, :, place]
            row_own[c, h : h + 1, :] = jnp.sum(product, axis=0, keepdims=True)

        for d in range(1, reach + 1):
            @pl.when(has_earlier(d))
            def _():
                for copy in grad_copies(c, d):
                    copy.start()

        for d in range(reach + 1):
            def query_part():
                for kv in range(kv_heads):
                    for h in range(kv * groups, (kv + 1) * groups):
                        g = g_own[lanes(h), place]
                        probs = p_own[h, d, :, place]
                        slope = dot(value_block(d)[:, lanes(kv)], g) - row_own[c, h : h + 1, :]
                        low = (probs.astype(jnp.float32) * slope).astype(jnp.bfloat16)
                        part = dot(k_turn[kv, d], low)
                        if d == 0:
                            dq_acc[h] = part
                            dk_acc[kv] += dot(low, q_ref[place, lanes(h)])
                            dv_acc[kv] += dot_nt(probs, g)
                        else:
                            dq_acc[h] += part
            on_earlier(d, query_part)
        for h in range(heads):
            dq_ref[place, lanes(h)] = (dq_acc[h] * score_scale).T.astype(jnp.bfloat16)

    late_keys(chunks - 1)
    for kv in range(kv_heads):
        lane = slice(kv * HEAD_SIZE, (kv + 1) * HEAD_SIZE)
        dk_ref[:, lane] = (dk_acc[kv] * score_scale).astype(jnp.bfloat16)
        dv_ref[:, lane] = dv_acc[kv].astype(jnp.bfloat16)

    for o in range(1, n_fsdp):
        w_copy(o).wait_send()
    if lean:
        @pl.when(gives_far)
        def _():
            far_first().wait_send()

        @pl.when(holds_far)
        def _():
            for d in range(1, n_seq):
                far_share(d).wait_send()
            for d in range(n_seq):
                far_pass(d).wait_send()

        @pl.when(is_helper)
        def _():
            for c in range(chunks):
                part_copy(c).wait_send()

    for c in range(chunks):
        for s in range(hops - 1):
            @pl.when(right_sends(s))
            def _():
                right_copy(c, s).wait_send()

            @pl.when(left_sends(s))
            def _():
                left_copy(c, s).wait_send()
    for d in range(1, reach + 1):
        @pl.when(has_later(d))
        def _():
            for copy in key_copies(d):
                copy.wait_send()

        @pl.when(has_earlier(d))
        def _():
            query_copy(d).wait_send()
            lse_copy(d).wait_send()
            for c in range(chunks):
                for copy in grad_copies(c, d):
                    copy.wait_send()


def place_kernel(a_in, b_in, c_in, a_out, b_out, c_out, sems):
    copies = [
        pltpu.make_async_copy(src, dst, sems.at[i])
        for i, (src, dst) in enumerate(((a_in, a_out), (b_in, b_out), (c_in, c_out)))
    ]
    for copy in copies:
        copy.start()
    for copy in copies:
        copy.wait()


def per_device(mesh, queries, keys, values, cotangent, out_weight):
    n_seq, n_tensor, n_fsdp = mesh.shape["seq"], mesh.shape["tensor"], mesh.shape["fsdp"]
    q, k, v, c = queries[0], keys[0], values[0], cotangent[0].T
    rows = q.shape[0]
    reach = min(WINDOW // rows, n_seq - 1)
    lean = is_lean(n_seq, n_tensor, n_fsdp, reach)
    heads, kv_heads = q.shape[1] // HEAD_SIZE, k.shape[1] // HEAD_SIZE
    chunks = rows // CHUNK
    bf16, f32 = jnp.bfloat16, jnp.float32
    vmem = pl.BlockSpec(memory_space=pltpu.VMEM)
    hbm = pl.BlockSpec(memory_space=pl.ANY)
    dma = pltpu.SemaphoreType.DMA
    dq, dk, dv = pl.pallas_call(
        functools.partial(kernel, n_seq, n_tensor, n_fsdp, reach),
        out_shape=[jax.ShapeDtypeStruct(x.shape, bf16) for x in (q, k, v)],
        in_specs=[vmem, vmem, vmem, hbm, hbm],
        out_specs=[vmem] * 3,
        scratch_shapes=[
            pltpu.VMEM((n_tensor * c.shape[0], rows), bf16),
            pltpu.VMEM((n_fsdp,) + out_weight.shape, bf16),
            pltpu.VMEM((reach,) + k.shape, bf16),
            pltpu.VMEM((reach,) + v.shape, bf16),
            pltpu.VMEM((reach,) + q.shape, bf16),
            pltpu.VMEM((8, rows), f32),
            pltpu.VMEM((reach, 8, rows), f32),
            pltpu.VMEM((chunks, 8, CHUNK), f32),
            pltpu.VMEM((chunks, reach, 8, CHUNK), f32),
            pltpu.VMEM(q.shape[::-1], bf16),
            pltpu.VMEM((reach,) + q.shape[::-1], bf16),
            pltpu.VMEM((heads, reach + 1, rows, rows), f32),
            pltpu.VMEM((heads, reach + 1, rows, rows), bf16),
            pltpu.VMEM((heads, reach, rows, rows), bf16),
            pltpu.VMEM((heads, HEAD_SIZE, rows), f32),
            pltpu.VMEM((kv_heads, reach + 1, HEAD_SIZE, rows), bf16),
            pltpu.VMEM((kv_heads, reach + 1, HEAD_SIZE, rows), bf16),
            pltpu.VMEM((heads, 1, rows), f32),
            pltpu.VMEM((heads, 1, rows), f32),
            pltpu.VMEM((heads, HEAD_SIZE, CHUNK), f32),
            pltpu.VMEM((kv_heads, rows, HEAD_SIZE), f32),
            pltpu.VMEM((kv_heads, rows, HEAD_SIZE), f32),
            pltpu.VMEM(out_weight.shape if lean else (16, 128), bf16),
            pltpu.VMEM((out_weight.shape[0], rows) if lean else (16, 128), bf16),
            pltpu.VMEM((out_weight.shape[0], rows) if lean else (16, 128), bf16),
            dma, dma,
            dma((n_fsdp,)), dma((n_fsdp,)),
            dma((chunks, n_tensor)), dma((chunks, n_tensor)),
            dma((chunks, n_tensor)), dma((chunks, n_tensor)),
            dma((3, reach + 1)), dma((3, reach + 1)),
            dma((reach + 1,)), dma((reach + 1,)),
            dma((2, chunks, reach + 1)), dma((2, chunks, reach + 1)),
            dma((n_seq,)), dma((n_seq,)), dma((n_seq,)), dma((n_seq,)), dma((chunks,)), dma((chunks,)),
        ],
        compiler_params=pltpu.CompilerParams(
            collective_id=0, has_side_effects=True, vmem_limit_bytes=56 * 2**20
        ),
        cost_estimate=pl.CostEstimate(flops=4 * 10**9, bytes_accessed=8 * 10**6, transcendentals=4 * 10**6),
    )(q, k, v, c, out_weight)
    dq, dk, dv = pl.pallas_call(
        place_kernel,
        out_shape=[jax.ShapeDtypeStruct(x.shape, bf16) for x in (q, k, v)],
        in_specs=[vmem] * 3,
        out_specs=[hbm] * 3,
        scratch_shapes=[dma((3,))],
    )(dq, dk, dv)
    return dq[None], dk[None], dv[None]


def solution(mesh):
    parts = P("fsdp", "seq", "tensor")
    return jax.shard_map(
        functools.partial(per_device, mesh),
        mesh=mesh,
        in_specs=(parts, parts, parts, parts, P("tensor", "fsdp")),
        out_specs=(parts, parts, parts),
        check_vma=False,
    )
```

```python
import functools

import jax
import jax.numpy as jnp
from jax import lax
from jax.experimental import pallas as pl
from jax.experimental.pallas import tpu as pltpu
from jax.sharding import PartitionSpec as P

HEAD_SIZE = 128
WINDOW = 1024
CHUNK = 128

score_scale = 168.0 ** (-0.5)
masked_score = -1e30
MESH = pl.DeviceIdType.MESH
NT = (((1,), (1,)), ((), ()))


def dot(a, b):
    return jnp.dot(a, b, preferred_element_type=jnp.float32)


def dot_nt(a, b):
    return lax.dot_general(a, b, NT, preferred_element_type=jnp.float32)


def is_lean(n_seq, n_tensor, n_fsdp, reach):
    return False


def kernel(
    n_seq, n_tensor, n_fsdp, reach,
    q_ref, k_ref, v_ref, c_ref, w_ref,
    dq_ref, dk_ref, dv_ref,
    c_all, w_all, k_in, v_in, q_in, lse_own, lse_in, row_own, row_in, g_own, g_in,
    s_buf, p_own, p_late, att, k_turn, v_turn, top, total, dq_acc, dk_acc, dv_acc,
    w_far, part_out, part_in,
    c_loc, w_loc, w_send, w_recv, right_send, right_recv, left_send, left_recv,
    kv_send, kv_recv, lse_send, lse_recv, g_send, g_recv,
    far_send, far_recv, pass_send, pass_recv, part_send, part_recv,
):
    rows = q_ref.shape[0]
    kv_heads = k_ref.shape[1] // HEAD_SIZE
    groups = q_ref.shape[1] // k_ref.shape[1]
    heads = kv_heads * groups
    chunks = rows // CHUNK
    features = c_ref.shape[0]
    fsdp_features = w_ref.shape[1]
    me_s, me_t, me_f = lax.axis_index("seq"), lax.axis_index("tensor"), lax.axis_index("fsdp")

    def seq_at(offset):
        return {"seq": lax.rem(me_s + offset + n_seq, n_seq)}

    def tensor_at(offset):
        return {"tensor": lax.rem(me_t + offset + n_tensor, n_tensor)}

    def fsdp_at(offset):
        return {"fsdp": lax.rem(me_f + offset + n_fsdp, n_fsdp)}

    seq_offsets = sorted({d % n_seq for r in range(1, reach + 1) for d in (r, -r)} - {0})
    tensor_offsets = sorted({1 % n_tensor, (n_tensor - 1) % n_tensor} - {0})
    peers = (
        [seq_at(d) for d in seq_offsets]
        + [tensor_at(d) for d in tensor_offsets]
        + [fsdp_at(d) for d in range(1, n_fsdp)]
    )
    barrier = pltpu.get_barrier_semaphore()
    for peer in peers:
        pl.semaphore_signal(barrier, inc=1, device_id=peer, device_id_type=MESH)
    pl.semaphore_wait(barrier, len(peers))

    def remote(src, dst, send, recv, peer):
        return pltpu.make_async_remote_copy(
            src_ref=src, dst_ref=dst, send_sem=send, recv_sem=recv,
            device_id=peer, device_id_type=MESH,
        )

    def has_earlier(d):
        return me_s >= d

    def has_later(d):
        return me_s + d < n_seq

    def block(slot):
        return pl.ds(pl.multiple_of(slot * features, 16), features)

    def right_copy(c, s):
        place = pl.ds(c * CHUNK, CHUNK)
        slot = lax.rem(me_t - s + n_tensor, n_tensor)
        there = c_all.at[c, block(slot)]
        src = c_ref.at[:, place] if s == 0 else there
        return remote(src, there, right_send.at[c, s], right_recv.at[c, s], tensor_at(1))

    def left_copy(c, s):
        place = pl.ds(c * CHUNK, CHUNK)
        slot = lax.rem(me_t + s, n_tensor)
        there = c_all.at[c, block(slot)]
        src = c_ref.at[:, place] if s == 0 else there
        return remote(src, there, left_send.at[c, s], left_recv.at[c, s], tensor_at(-1))

    lean = is_lean(n_seq, n_tensor, n_fsdp, reach)
    is_end = (me_t == 0) | (me_t == 3)
    is_helper = (me_t == 1) | (me_t == 2)
    far_shard = 1 - lax.div(me_t, 2)
    gives_far = is_end & (me_f == far_shard)
    holds_far = is_helper & (me_f == far_shard)
    takes_far = is_helper & (me_f != far_shard)

    def far_rows(offset):
        quarter = w_ref.shape[0] // n_seq
        piece = lax.rem(me_s - offset + n_seq, n_seq)
        return pl.ds(pl.multiple_of(piece * quarter, 16), quarter)

    def far_first():
        place = far_rows(0)
        return remote(w_ref.at[place], w_far.at[place], far_send.at[0], far_recv.at[0],
                      {"tensor": 1 + lax.div(me_t, 3)})

    def far_share(d):
        place = far_rows(0)
        return remote(w_far.at[place], w_far.at[place], far_send.at[d], far_recv.at[d], seq_at(d))

    def far_pass(d):
        place = far_rows(d)
        return remote(w_far.at[place], w_far.at[place], pass_send.at[d], pass_recv.at[d], fsdp_at(1))

    def part_copy(c):
        place = pl.ds(c * CHUNK, CHUNK)
        return remote(part_out.at[:, place], part_in.at[:, place], part_send.at[c], part_recv.at[c],
                      {"tensor": 3 * lax.div(me_t, 2)})

    def right_sends(s):
        if lean and s > 0:
            return me_t == 1
        return (me_t + 1 < n_tensor) & (me_t >= s)

    def left_sends(s):
        if lean and s > 0:
            return me_t == 2
        return (me_t >= 1) & (me_t + s < n_tensor)

    def right_lands(s):
        return me_t == 2 if lean and s > 1 else me_t >= s

    def left_lands(s):
        return me_t == 1 if lean and s > 1 else me_t + s < n_tensor

    hops = 3 if lean else n_tensor

    def w_copy(o):
        return remote(w_ref, w_all.at[me_f], w_send.at[o], w_recv.at[o], fsdp_at(o))

    def key_copies(d):
        return [
            remote(k_ref, k_in.at[d - 1], kv_send.at[0, d], kv_recv.at[0, d], seq_at(d)),
            remote(v_ref, v_in.at[d - 1], kv_send.at[1, d], kv_recv.at[1, d], seq_at(d)),
        ]

    def query_copy(d):
        return remote(q_ref, q_in.at[d - 1], kv_send.at[2, d], kv_recv.at[2, d], seq_at(-d))

    def lse_copy(d):
        return remote(lse_own, lse_in.at[d - 1], lse_send.at[d], lse_recv.at[d], seq_at(-d))

    def grad_copies(c, d):
        place = pl.ds(c * CHUNK, CHUNK)
        return [
            remote(g_own.at[:, place], g_in.at[d - 1, :, place], g_send.at[0, c, d], g_recv.at[0, c, d], seq_at(-d)),
            remote(row_own.at[c], row_in.at[c, d - 1], g_send.at[1, c, d], g_recv.at[1, c, d], seq_at(-d)),
        ]

    for c in range(chunks):
        @pl.when(right_sends(0))
        def _():
            right_copy(c, 0).start()

        @pl.when(left_sends(0))
        def _():
            left_copy(c, 0).start()

        if lean and c == 0:
            @pl.when(gives_far)
            def _():
                far_first().start()
    for o in range(1, n_fsdp):
        w_copy(o).start()
    for d in range(1, reach + 1):
        @pl.when(has_later(d))
        def _():
            for copy in key_copies(d):
                copy.start()

        @pl.when(has_earlier(d))
        def _():
            query_copy(d).start()

    def pump(c, s):
        @pl.when(right_lands(s))
        def _():
            right_copy(c, s - 1).wait_recv()

        if s < hops - 1:
            @pl.when(right_sends(s))
            def _():
                right_copy(c, s).start()

        @pl.when(left_lands(s))
        def _():
            left_copy(c, s - 1).wait_recv()

        if s < hops - 1:
            @pl.when(left_sends(s))
            def _():
                left_copy(c, s).start()

    pumped = []

    def pump_next(count):
        order = [(c, s) for s in range(1, min(3, hops)) for c in range(chunks)]
        order += [(c, s) for c in range(chunks) for s in range(3, hops)]
        for c, s in order[len(pumped) : len(pumped) + count]:
            pump(c, s)
            pumped.append((c, s))

    own_c = [
        pltpu.make_async_copy(c_ref.at[:, pl.ds(c * CHUNK, CHUNK)], c_all.at[c, block(me_t)], c_loc.at[c])
        for c in range(chunks)
    ]
    for copy in own_c:
        copy.start()
    own_w = pltpu.make_async_copy(w_ref, w_all.at[me_f], w_loc)
    own_w.start()

    def lanes(h):
        return slice(h * HEAD_SIZE, (h + 1) * HEAD_SIZE)

    def key_block(d):
        return k_ref if d == 0 else k_in.at[d - 1]

    def value_block(d):
        return v_ref if d == 0 else v_in.at[d - 1]

    def on_earlier(d, do):
        if d == 0:
            do()
        else:
            pl.when(has_earlier(d))(do)

    def masked(scores, d):
        shape = (rows, rows)
        if d == 0:
            j, i = lax.broadcasted_iota(jnp.int32, shape, 0), lax.broadcasted_iota(jnp.int32, shape, 1)
            return jnp.where(j <= i, scores, masked_score)
        if (d + 1) * rows - 1 >= WINDOW:
            j, i = lax.broadcasted_iota(jnp.int32, shape, 0), lax.broadcasted_iota(jnp.int32, shape, 1)
            return jnp.where(j - i > d * rows - WINDOW, scores, masked_score)
        return scores

    pump_next(1)
    lse_own[...] = jnp.zeros_like(lse_own)
    row_own[...] = jnp.zeros_like(row_own)
    for d in range(1, reach + 1):
        @pl.when(has_earlier(d))
        def _():
            for copy in key_copies(d):
                copy.wait_recv()

    for d in range(reach + 1):
        def score():
            for kv in range(kv_heads):
                k_turn[kv, d] = key_block(d)[:, lanes(kv)].T
                v_turn[kv, d] = value_block(d)[:, lanes(kv)].T
            for h in range(heads):
                scores = masked(dot_nt(key_block(d)[:, lanes(h // groups)], q_ref[:, lanes(h)]) * score_scale, d)
                s_buf[h, d] = scores
                high = jnp.max(scores, axis=0, keepdims=True)
                top[h] = high if d == 0 else jnp.maximum(top[h], high)
        on_earlier(d, score)
    pump_next(1)
    for d in range(reach + 1):
        def add():
            for h in range(heads):
                powers = jnp.exp(s_buf[h, d] - top[h])
                part = jnp.sum(powers, axis=0, keepdims=True)
                total[h] = part if d == 0 else total[h] + part
        on_earlier(d, add)
    for h in range(heads):
        lse_own[h : h + 1, :] = top[h] + jnp.log(total[h])
    for d in range(1, reach + 1):
        @pl.when(has_earlier(d))
        def _():
            lse_copy(d).start()

    for d in range(reach + 1):
        def spread():
            for h in range(heads):
                low = jnp.exp(s_buf[h, d] - lse_own[h : h + 1, :]).astype(jnp.bfloat16)
                p_own[h, d] = low
                part = dot(v_turn[h // groups, d], low)
                att[h] = part if d == 0 else att[h] + part
        on_earlier(d, spread)

    if lean:
        @pl.when(holds_far)
        def _():
            far_first().wait_recv()
            for d in range(1, n_seq):
                far_share(d).start()
            far_pass(0).start()

    own_w.wait()
    for o in range(1, n_fsdp):
        w_copy(o).wait_recv()
    pump_next(1)

    for d in range(1, reach + 1):
        @pl.when(has_later(d))
        def _():
            query_copy(d).wait_recv()
            lse_copy(d).wait_recv()

            for h in range(heads):
                scores = masked(dot_nt(k_ref[:, lanes(h // groups)], q_in[d - 1, :, lanes(h)]) * score_scale, d)
                p_late[h, d - 1] = jnp.exp(scores - lse_in[d - 1, h : h + 1, :]).astype(jnp.bfloat16)

    if lean:
        @pl.when(holds_far)
        def _():
            for d in range(1, n_seq):
                far_share(d).wait_recv()
                far_pass(d).start()

        @pl.when(takes_far)
        def _():
            for d in range(n_seq):
                far_pass(d).wait_recv()

    dk_acc[...] = jnp.zeros_like(dk_acc)
    dv_acc[...] = jnp.zeros_like(dv_acc)
    for copy in own_c:
        copy.wait()

    def late_keys(c):
        place = pl.ds(c * CHUNK, CHUNK)
        for d in range(1, reach + 1):
            @pl.when(has_later(d))
            def _():
                for copy in grad_copies(c, d):
                    copy.wait_recv()

                for kv in range(kv_heads):
                    k_part, v_part = dk_acc[kv], dv_acc[kv]
                    for h in range(kv * groups, (kv + 1) * groups):
                        g = g_in[d - 1, lanes(h), place]
                        probs = p_late[h, d - 1, :, place]
                        slope = dot(v_ref[:, lanes(kv)], g) - row_in[c, d - 1, h : h + 1, :]
                        low = (probs.astype(jnp.float32) * slope).astype(jnp.bfloat16)
                        k_part += dot(low, q_in[d - 1, place, lanes(h)])
                        v_part += dot_nt(probs, g)
                    dk_acc[kv], dv_acc[kv] = k_part, v_part

    for c in range(chunks):
        place = pl.ds(c * CHUNK, CHUNK)
        if c > 0:
            late_keys(c - 1)
        while not all((c, s) in pumped for s in range(1, hops)):
            pump_next(1)
        def full_sums():
            sums = dot(w_all[0], c_all[c, :fsdp_features])
            for f in range(1, n_fsdp):
                sums += dot(w_all[f], c_all[c, f * fsdp_features : (f + 1) * fsdp_features])
            g_own[:, place] = sums.astype(jnp.bfloat16)

        def shard_features(f):
            return pl.ds(pl.multiple_of(f * fsdp_features, 16), fsdp_features)

        if lean:
            @pl.when(is_helper)
            def _():
                part = dot(w_far[...], c_all[c, shard_features(far_shard)])
                part_out[:, place] = part.astype(jnp.bfloat16)
                part_copy(c).start()
                full_sums()

            @pl.when(is_end)
            def _():
                near = 1 - far_shard
                sums = dot(w_all[near], c_all[c, shard_features(near)])
                part_copy(c).wait_recv()
                g_own[:, place] = (sums + part_in[:, place].astype(jnp.float32)).astype(jnp.bfloat16)
        else:
            full_sums()

        for h in range(heads):
            product = g_own[lanes(h), place].astype(jnp.float32) * att[h, :, place]
            row_own[c, h : h + 1, :] = jnp.sum(product, axis=0, keepdims=True)

        for d in range(1, reach + 1):
            @pl.when(has_earlier(d))
            def _():
                for copy in grad_copies(c, d):
                    copy.start()

        for d in range(reach + 1):
            def query_part():
                for kv in range(kv_heads):
                    for h in range(kv * groups, (kv + 1) * groups):
                        g = g_own[lanes(h), place]
                        probs = p_own[h, d, :, place]
                        slope = dot(value_block(d)[:, lanes(kv)], g) - row_own[c, h : h + 1, :]
                        low = (probs.astype(jnp.float32) * slope).astype(jnp.bfloat16)
                        part = dot(k_turn[kv, d], low)
                        if d == 0:
                            dq_acc[h] = part
                            dk_acc[kv] += dot(low, q_ref[place, lanes(h)])
                            dv_acc[kv] += dot_nt(probs, g)
                        else:
                            dq_acc[h] += part
            on_earlier(d, query_part)
        for h in range(heads):
            dq_ref[place, lanes(h)] = (dq_acc[h] * score_scale).T.astype(jnp.bfloat16)

    late_keys(chunks - 1)
    for kv in range(kv_heads):
        lane = slice(kv * HEAD_SIZE, (kv + 1) * HEAD_SIZE)
        dk_ref[:, lane] = (dk_acc[kv] * score_scale).astype(jnp.bfloat16)
        dv_ref[:, lane] = dv_acc[kv].astype(jnp.bfloat16)

    for o in range(1, n_fsdp):
        w_copy(o).wait_send()
    if lean:
        @pl.when(gives_far)
        def _():
            far_first().wait_send()

        @pl.when(holds_far)
        def _():
            for d in range(1, n_seq):
                far_share(d).wait_send()
            for d in range(n_seq):
                far_pass(d).wait_send()

        @pl.when(is_helper)
        def _():
            for c in range(chunks):
                part_copy(c).wait_send()

    for c in range(chunks):
        for s in range(hops - 1):
            @pl.when(right_sends(s))
            def _():
                right_copy(c, s).wait_send()

            @pl.when(left_sends(s))
            def _():
                left_copy(c, s).wait_send()
    for d in range(1, reach + 1):
        @pl.when(has_later(d))
        def _():
            for copy in key_copies(d):
                copy.wait_send()

        @pl.when(has_earlier(d))
        def _():
            query_copy(d).wait_send()
            lse_copy(d).wait_send()
            for c in range(chunks):
                for copy in grad_copies(c, d):
                    copy.wait_send()


def place_kernel(a_in, b_in, c_in, a_out, b_out, c_out, sems):
    copies = [
        pltpu.make_async_copy(src, dst, sems.at[i])
        for i, (src, dst) in enumerate(((a_in, a_out), (b_in, b_out), (c_in, c_out)))
    ]
    for copy in copies:
        copy.start()
    for copy in copies:
        copy.wait()


def per_device(mesh, queries, keys, values, cotangent, out_weight):
    n_seq, n_tensor, n_fsdp = mesh.shape["seq"], mesh.shape["tensor"], mesh.shape["fsdp"]
    q, k, v, c = queries[0], keys[0], values[0], cotangent[0].T
    rows = q.shape[0]
    reach = min(WINDOW // rows, n_seq - 1)
    lean = is_lean(n_seq, n_tensor, n_fsdp, reach)
    heads, kv_heads = q.shape[1] // HEAD_SIZE, k.shape[1] // HEAD_SIZE
    chunks = rows // CHUNK
    bf16, f32 = jnp.bfloat16, jnp.float32
    vmem = pl.BlockSpec(memory_space=pltpu.VMEM)
    hbm = pl.BlockSpec(memory_space=pl.ANY)
    dma = pltpu.SemaphoreType.DMA
    dq, dk, dv = pl.pallas_call(
        functools.partial(kernel, n_seq, n_tensor, n_fsdp, reach),
        out_shape=[jax.ShapeDtypeStruct(x.shape, bf16) for x in (q, k, v)],
        in_specs=[vmem, vmem, vmem, hbm, hbm],
        out_specs=[vmem] * 3,
        scratch_shapes=[
            pltpu.VMEM((chunks, n_tensor * c.shape[0], CHUNK), bf16),
            pltpu.VMEM((n_fsdp,) + out_weight.shape, bf16),
            pltpu.VMEM((reach,) + k.shape, bf16),
            pltpu.VMEM((reach,) + v.shape, bf16),
            pltpu.VMEM((reach,) + q.shape, bf16),
            pltpu.VMEM((8, rows), f32),
            pltpu.VMEM((reach, 8, rows), f32),
            pltpu.VMEM((chunks, 8, CHUNK), f32),
            pltpu.VMEM((chunks, reach, 8, CHUNK), f32),
            pltpu.VMEM(q.shape[::-1], bf16),
            pltpu.VMEM((reach,) + q.shape[::-1], bf16),
            pltpu.VMEM((heads, reach + 1, rows, rows), f32),
            pltpu.VMEM((heads, reach + 1, rows, rows), bf16),
            pltpu.VMEM((heads, reach, rows, rows), bf16),
            pltpu.VMEM((heads, HEAD_SIZE, rows), f32),
            pltpu.VMEM((kv_heads, reach + 1, HEAD_SIZE, rows), bf16),
            pltpu.VMEM((kv_heads, reach + 1, HEAD_SIZE, rows), bf16),
            pltpu.VMEM((heads, 1, rows), f32),
            pltpu.VMEM((heads, 1, rows), f32),
            pltpu.VMEM((heads, HEAD_SIZE, CHUNK), f32),
            pltpu.VMEM((kv_heads, rows, HEAD_SIZE), f32),
            pltpu.VMEM((kv_heads, rows, HEAD_SIZE), f32),
            pltpu.VMEM(out_weight.shape if lean else (16, 128), bf16),
            pltpu.VMEM((out_weight.shape[0], rows) if lean else (16, 128), bf16),
            pltpu.VMEM((out_weight.shape[0], rows) if lean else (16, 128), bf16),
            dma((chunks,)), dma,
            dma((n_fsdp,)), dma((n_fsdp,)),
            dma((chunks, n_tensor)), dma((chunks, n_tensor)),
            dma((chunks, n_tensor)), dma((chunks, n_tensor)),
            dma((3, reach + 1)), dma((3, reach + 1)),
            dma((reach + 1,)), dma((reach + 1,)),
            dma((2, chunks, reach + 1)), dma((2, chunks, reach + 1)),
            dma((n_seq,)), dma((n_seq,)), dma((n_seq,)), dma((n_seq,)), dma((chunks,)), dma((chunks,)),
        ],
        compiler_params=pltpu.CompilerParams(
            collective_id=0, has_side_effects=True, vmem_limit_bytes=56 * 2**20
        ),
        cost_estimate=pl.CostEstimate(flops=4 * 10**9, bytes_accessed=8 * 10**6, transcendentals=4 * 10**6),
    )(q, k, v, c, out_weight)
    dq, dk, dv = pl.pallas_call(
        place_kernel,
        out_shape=[jax.ShapeDtypeStruct(x.shape, bf16) for x in (q, k, v)],
        in_specs=[vmem] * 3,
        out_specs=[hbm] * 3,
        scratch_shapes=[dma((3,))],
    )(dq, dk, dv)
    return dq[None], dk[None], dv[None]


def solution(mesh):
    parts = P("fsdp", "seq", "tensor")
    return jax.shard_map(
        functools.partial(per_device, mesh),
        mesh=mesh,
        in_specs=(parts, parts, parts, parts, P("tensor", "fsdp")),
        out_specs=(parts, parts, parts),
        check_vma=False,
    )
```
